256 devices in a mesh: ctx: 16 (over z, core), head: 16 (over y, x).
Axes of the slice: x: 4, y: 4, z: 8, core: 2. Of those that a mesh axis runs over, the one named last changes fastest.
Arguments:
- stretch_keys: bfloat16 [16, 65536, 128], P('head', 'ctx'), may hold values from -6 to 6
- stretch_values: bfloat16 [16, 65536, 128], P('head', 'ctx'), may hold values from -6 to 6
- stretch_assign: int32 [16, 65536], P('head', 'ctx'), may hold values from 0 to 4095, as said below
- centroid_keys: float32 [16, 4096, 128], P('head'), may hold values from -3.5 to 3.5
- centroid_values: float32 [16, 4096, 128], P('head'), may hold values from -3 to 3
- cluster_counts: float32 [16, 4096], P('head'), may hold values from 64 to 1024
- cache_keys: bfloat16 [16, 131072, 128], P('head', 'ctx'), may hold values from -6 to 6
- cache_values: bfloat16 [16, 131072, 128], P('head', 'ctx'), may hold values from -6 to 6
- block_cluster: int32 [16, 8192], P('head', 'ctx'), may hold values from 0 to 4095
- selected: int32 [4, 16, 64], P(None, 'head'), may hold values from 0 to 4095
- queries: bfloat16 [4, 64, 16, 128], P(None, 'head'), may hold values from -90 to 90
Outputs:
- new_keys: float32 [16, 4096, 128], P('head', 'ctx')
- new_values: float32 [16, 4096, 128], P('head', 'ctx')
- new_counts: float32 [16, 4096], P('head', 'ctx')
- attended: bfloat16 [4, 16, 64, 128], P(None, 'head', 'ctx')
The draws below stay inside these ranges and needn't reach their ends.
Inputs may be any that keep to these rules, and one draw needn't show every extreme that they name: `stretch_assign`: within each aligned block of 4096 prefill positions of one head, the clusters of one group j // (4096 / 16) are named at most 320 times; in every block some group is named exactly 320 times.
All inputs are finite; a program needn't handle non-finite values.
Results may differ from the reference program's by a relative error of at most 0.0045.
Values may be sent and summed in bfloat16 or wider, within the bound.
A program may use at most 128 MiB of HBM per device.

```python
import math
import jax
import jax.numpy as jnp
from jax import lax

HD = 128
CLUSTERS = 4096
TOK_DEV = 4096
BLK = 16
SEL = 64
STEPS = 4
QROWS = 64
HEADS = 16
STRETCH = 65536
CONTEXT = 131072
NBLK = 8192
N_CTX = 16


def paired_draw(key):
    first = jax.random.fold_in(key, 11)
    second = jax.random.fold_in(key, 12)
    centre = jnp.clip(0.3 * jax.random.normal(first, (HEADS, CLUSTERS, HD), jnp.float32), -1.8, 1.8)
    query = jnp.clip(3.5 * jax.random.normal(second, (STEPS, QROWS, HEADS, HD), jnp.float32), -21.0, 21.0)
    return (centre, query)


def draw_centroid_keys(key, part):
    centre, query = paired_draw(key)
    return centre


def draw_queries(key, part):
    centre, query = paired_draw(key)
    return query.astype(jnp.bfloat16)


def assign_block(key):
    base = TOK_DEV // N_CTX
    extra = TOK_DEV // (4 * N_CTX)
    owned = CLUSTERS // N_CTX
    key_heavy, key_light, key_order, key_inner = jax.random.split(key, 4)
    heavy = jax.random.randint(key_heavy, (), 0, N_CTX, dtype=jnp.int32)
    light = (heavy + jax.random.randint(key_light, (), 1, N_CTX, dtype=jnp.int32)) % N_CTX
    owners = jnp.arange(N_CTX, dtype=jnp.int32)
    amounts = base + extra * (owners == heavy).astype(jnp.int32) - extra * (owners == light).astype(jnp.int32)
    bounds = jnp.cumsum(amounts)
    positions = jnp.arange(TOK_DEV, dtype=jnp.int32)
    owner = jnp.sum((positions[:, None] >= bounds[None, :]).astype(jnp.int32), axis=1)
    owner = jax.random.permutation(key_order, owner)
    inner = jax.random.randint(key_inner, (TOK_DEV,), 0, owned, dtype=jnp.int32)
    return owner * owned + inner


def draw_stretch_assign(key, part):
    keys = jax.random.split(jax.random.fold_in(key, 21), HEADS * N_CTX)
    return jax.vmap(assign_block)(keys).reshape(HEADS, STRETCH)


def place_ends(result, rng, smallest, top_value):
    longest = result.shape.index(max(result.shape))
    spots = []
    for shift in (0, 1):
        where = [jax.random.randint(jax.random.fold_in(rng, axis), (), 0, length) for axis, length in enumerate(result.shape)]
        where[longest] = (where[longest] + shift) % result.shape[longest]
        spots.append(tuple(where))
    return result.at[spots[0]].set(smallest).at[spots[1]].set(top_value)


def shard_levels(stream_key, dims, cuts, smallest, high):
    def one(axis_at, shards_of):
        heights = jax.random.uniform(jax.random.fold_in(jax.random.fold_in(stream_key, 6), axis_at), (shards_of,), jnp.float32, smallest / len(cuts), high / len(cuts))
        return jnp.repeat(jnp.exp(heights), dims[axis_at] // shards_of).reshape((-1,) + (1,) * (len(dims) - axis_at - 1))

    gain = one(*cuts[0])
    for cut in cuts[1:]:
        gain = gain * one(*cut)
    return gain


def normal_values(stream_key, shape, deviation, most, pieces=(), held_as=jnp.bfloat16):
    values = deviation * jax.random.normal(stream_key, shape, jnp.float32)
    if pieces:
        values = values * shard_levels(stream_key, shape, pieces, -0.22, 0.18)
    return jnp.clip(values, -most, most).astype(held_as)


def setup_inputs(seed: int = 0) -> dict:
    key_list = jax.random.split(jax.random.key(seed), 12)
    stretch_keys = normal_values(key_list[0], (HEADS, STRETCH, HD), 1.0, 6.0, ((0, 16), (1, 16)))
    stretch_values = normal_values(key_list[1], (HEADS, STRETCH, HD), 1.0, 6.0, ((0, 16), (1, 16)))
    stretch_assign = draw_stretch_assign(jax.random.fold_in(key_list[11], 71), 0)
    centroid_keys = draw_centroid_keys(jax.random.fold_in(key_list[11], 71), 0)
    centroid_values = normal_values(key_list[4], (HEADS, CLUSTERS, HD), 0.5, 3.0, ((0, 16),), jnp.float32)
    cluster_counts = jnp.clip(jnp.exp(math.log(1024.0) - 2.7725887 * jax.random.uniform(key_list[5], (HEADS, CLUSTERS), jnp.float32) ** shard_levels(key_list[5], (HEADS, CLUSTERS), ((0, 16),), -0.2, 0.2)), 64.0, 1024.0)
    cache_keys = normal_values(key_list[6], (HEADS, CONTEXT, HD), 1.0, 6.0, ((0, 16), (1, 16)))
    cache_values = normal_values(key_list[7], (HEADS, CONTEXT, HD), 1.0, 6.0, ((0, 16), (1, 16)))
    block_cluster = place_ends(jax.random.randint(key_list[8], (HEADS, NBLK), 0, CLUSTERS), jax.random.fold_in(key_list[8], 1), 0, CLUSTERS - 1).astype(jnp.int32)
    selected = place_ends(jax.random.randint(key_list[9], (STEPS, HEADS, SEL), 0, CLUSTERS), jax.random.fold_in(key_list[9], 1), 0, CLUSTERS - 1).astype(jnp.int32)
    queries = draw_queries(jax.random.fold_in(key_list[11], 71), 0)
    return {"stretch_keys": stretch_keys, "stretch_values": stretch_values, "stretch_assign": stretch_assign, "centroid_keys": centroid_keys, "centroid_values": centroid_values, "cluster_counts": cluster_counts, "cache_keys": cache_keys, "cache_values": cache_values, "block_cluster": block_cluster, "selected": selected, "queries": queries}


def one_head(items):
    stretch_k, stretch_v, assign, cent_k, cent_v, counts, cache_k, cache_v, blocks, chosen, rows_q = items
    joined = jnp.concatenate([stretch_k, stretch_v], axis=1).astype(jnp.float32)
    sums = jax.ops.segment_sum(joined, assign, num_segments=CLUSTERS)
    added = jax.ops.segment_sum(jnp.ones(assign.shape, jnp.float32), assign, num_segments=CLUSTERS)
    total = counts + added
    new_k = (counts[:, None] * cent_k + sums[:, :HD]) / total[:, None]
    new_v = (counts[:, None] * cent_v + sums[:, HD:]) / total[:, None]
    block_hit = jnp.any(blocks[None, :, None] == chosen[:, None, :], axis=-1)
    cache_hit = jnp.repeat(block_hit, BLK, axis=1)
    stretch_hit = jnp.any(assign[None, :, None] == chosen[:, None, :], axis=-1)
    labels = jnp.arange(CLUSTERS, dtype=jnp.int32)
    centre_free = jnp.logical_not(jnp.any(labels[None, :, None] == chosen[:, None, :], axis=-1))
    scale = HD ** (-0.5)
    hp = lax.Precision.HIGHEST
    query = rows_q.astype(jnp.float32)
    s_cache = jnp.einsum('sqd,td->sqt', query, cache_k.astype(jnp.float32), precision=hp) * scale
    s_stretch = jnp.einsum('sqd,td->sqt', query, stretch_k.astype(jnp.float32), precision=hp) * scale
    s_centre = jnp.einsum('sqd,cd->sqc', query, new_k, precision=hp) * scale + jnp.log(total)[None, None, :]
    s_cache = jnp.where(cache_hit[:, None, :], s_cache, -1e+30)
    s_stretch = jnp.where(stretch_hit[:, None, :], s_stretch, -1e+30)
    s_centre = jnp.where(centre_free[:, None, :], s_centre, -1e+30)
    peak = jnp.maximum(jnp.maximum(jnp.max(s_cache, -1), jnp.max(s_stretch, -1)), jnp.max(s_centre, -1))
    p_cache = jnp.where(cache_hit[:, None, :], jnp.exp(s_cache - peak[..., None]), 0.0)
    p_stretch = jnp.where(stretch_hit[:, None, :], jnp.exp(s_stretch - peak[..., None]), 0.0)
    p_centre = jnp.where(centre_free[:, None, :], jnp.exp(s_centre - peak[..., None]), 0.0)
    whole = jnp.sum(p_cache, -1) + jnp.sum(p_stretch, -1) + jnp.sum(p_centre, -1)
    r_cache = lax.optimization_barrier(p_cache.astype(jnp.bfloat16)).astype(jnp.float32)
    r_stretch = lax.optimization_barrier(p_stretch.astype(jnp.bfloat16)).astype(jnp.float32)
    acc = jnp.einsum('sqt,td->sqd', r_cache, cache_v.astype(jnp.float32), precision=hp)
    acc = acc + jnp.einsum('sqt,td->sqd', r_stretch, stretch_v.astype(jnp.float32), precision=hp)
    acc = acc + jnp.einsum('sqc,cd->sqd', p_centre, new_v, precision=hp)
    out = (acc / whole[..., None]).astype(jnp.bfloat16)
    return (new_k, new_v, total, out)

def reference(stretch_keys, stretch_values, stretch_assign, centroid_keys, centroid_values, cluster_counts, cache_keys, cache_values, block_cluster, selected, queries):
    items = (stretch_keys, stretch_values, stretch_assign, centroid_keys, centroid_values, cluster_counts, cache_keys, cache_values, block_cluster, jnp.moveaxis(selected, 1, 0), jnp.moveaxis(queries, 2, 0))
    new_keys, new_values, new_counts, attended = lax.map(one_head, items)
    return (new_keys, new_values, new_counts, jnp.moveaxis(attended, 0, 1))
```

```python
import functools
import math

import jax
import jax.numpy as jnp
from jax import lax
from jax.experimental import pallas as pl
from jax.experimental.pallas import tpu as pltpu
from jax.sharding import PartitionSpec as P

MESH = pl.DeviceIdType.MESH
F32 = jnp.float32
BF16 = jnp.bfloat16
LOG2E = math.log2(math.e)
MASKED = -1e30
FLOOR = -1e29
TILE = 512
SEG = 1024
NT = (((1,), (1,)), ((), ()))


def split2(x):
    high = x.astype(BF16)
    return high, (x - high.astype(F32)).astype(BF16)


def split3(x):
    high = x.astype(BF16)
    rest = x - high.astype(F32)
    mid = rest.astype(BF16)
    return high, mid, (rest - mid.astype(F32)).astype(BF16)


def kernel(
    nctx, nhead, owned, steps, width,
    sel, assign, blocks, old_counts, queries, skeys, svals, ckeys, cvals, cent_k, cent_v,
    out_k, out_v, out_n, out_a,
    kv, cen, hits, bias, scores, mrun, acc, lrun, rel, part, own,
    sib_send, sib_recv, ring_send, ring_recv, qsend, qrecv, csend, crecv, fsend, frecv, lsend, lrecv,
    load_sem, q_ss, q_rs, c_ss, c_rs, s_ss, s_rs, r_ss, r_rs, f_ss, f_rs, l_ss, l_rs,
):
    me = lax.axis_index("ctx")
    head = lax.axis_index("head")
    z, core = me // 2, lax.rem(me, 2)
    nz = nctx // 2
    tokens = skeys.shape[1]
    cached = ckeys.shape[1]
    rows = queries.shape[0]
    share = rows // nctx
    stretch_tiles = tokens // TILE
    tiles = (tokens + cached) // TILE

    loads = [
        pltpu.make_async_copy(skeys.at[0], kv.at[pl.ds(0, tokens), pl.ds(0, width)], load_sem.at[0]),
        pltpu.make_async_copy(svals.at[0], kv.at[pl.ds(0, tokens), pl.ds(width, width)], load_sem.at[1]),
        pltpu.make_async_copy(ckeys.at[0], kv.at[pl.ds(tokens, cached), pl.ds(0, width)], load_sem.at[2]),
        pltpu.make_async_copy(cvals.at[0], kv.at[pl.ds(tokens, cached), pl.ds(width, width)], load_sem.at[3]),
        pltpu.make_async_copy(cent_k.at[0, pl.ds(me * owned, owned), :], cen.at[0], load_sem.at[4]),
        pltpu.make_async_copy(cent_v.at[0, pl.ds(me * owned, owned), :], cen.at[1], load_sem.at[5]),
    ]
    for load in loads:
        load.start()

    barrier = pltpu.get_barrier_semaphore()

    def greet(k, _):
        pl.semaphore_signal(barrier, inc=1, device_id={"ctx": lax.rem(me + k, nctx)}, device_id_type=MESH)
        return 0

    def greet_heads(k, _):
        pl.semaphore_signal(barrier, inc=1, device_id={"head": lax.rem(head + k, nhead)}, device_id_type=MESH)
        return 0

    lax.fori_loop(1, nctx, greet, 0)
    lax.fori_loop(1, nhead, greet_heads, 0)

    ids = assign[...]

    iota = lax.broadcasted_iota(jnp.int32, (owned, width), 0).astype(F32).astype(BF16)
    iota = iota.reshape(owned // 16, 16, width)

    def segment(j, offset):
        zd = lax.rem(z + offset, nz)
        rel[0] = (ids - owned * (2 * zd + 1 - core)).astype(F32)
        rel[1] = (ids - owned * (2 * zd + core)).astype(F32)
        part[...] = jnp.zeros_like(part)

        def step(n, _):
            hot = []
            for side in range(2):
                block = rel[side, pl.ds(pl.multiple_of(n * (SEG // 128), 8), SEG // 128), :]
                pieces = []
                for u in range(SEG // 128):
                    row = jnp.broadcast_to(block[u : u + 1, :], (16, 128)).astype(BF16)
                    equal = iota == row[None]
                    pieces.append(jnp.where(equal, jnp.ones((), BF16), jnp.zeros((), BF16)).reshape(owned, 128))
                hot.append(jnp.concatenate(pieces, axis=1))
            hot = jnp.concatenate(hot, axis=0)
            data = kv[pl.ds(pl.multiple_of(n * SEG, SEG), SEG), :]
            part[...] += jnp.dot(hot, data, preferred_element_type=F32)
            return 0

        lax.fori_loop(0, tokens // SEG, step, 0)
        sib_send[j] = part[0:owned, :].astype(BF16)
        own[j] = part[owned : 2 * owned, :]

    def sibling(j):
        return pltpu.make_async_remote_copy(
            sib_send.at[j], sib_recv.at[j], s_ss.at[j], s_rs.at[j],
            device_id={"ctx": 2 * z + 1 - core}, device_id_type=MESH,
        )

    def hop(direction, step, half):
        at = (direction * 4 + step) * 2 + half
        to = lax.rem(z + (1 if direction == 0 else nz - 1), nz)
        return pltpu.make_async_remote_copy(
            ring_send.at[at], ring_recv.at[at], r_ss.at[at], r_rs.at[at],
            device_id={"ctx": 2 * to + core}, device_id_type=MESH,
        )

    def mixed(j, half, arrivals):
        columns = slice(half * width, (half + 1) * width)
        value = own[j, :, columns] + sib_recv[j, :, columns].astype(F32)
        for direction, step in arrivals:
            hop(direction, step, half).wait_recv()
            value = value + ring_recv[(direction * 4 + step) * 2 + half].astype(F32)
        return value

    hops = []

    def forward(j, direction, step):
        sibling(j).wait_recv()
        first = 0 if direction == 0 else 1
        for half in (first, 1 - first):
            arrivals = []
            if step >= 2 or (step == 1 and half == first):
                arrivals = [(direction, step - 1)]
            ring_send[(direction * 4 + step) * 2 + half] = mixed(j, half, arrivals).astype(BF16)
            copy = hop(direction, step, half)
            copy.start()
            hops.append(copy)

    def start_ring():
        sibling(0).wait_recv()
        for direction in (0, 1):
            ring_send[direction * 8 + direction] = mixed(0, direction, []).astype(BF16)
            copy = hop(direction, 0, direction)
            copy.start()
            hops.append(copy)

    def query_copy(k):
        to = lax.rem(head + k, nhead)
        return pltpu.make_async_remote_copy(
            qsend.at[to], qrecv.at[head], q_ss.at[k], q_rs.at[k], device_id={"head": to}, device_id_type=MESH
        )

    def count_copy(k):
        to = lax.rem(me + k, nctx)
        return pltpu.make_async_remote_copy(
            csend.at[to], crecv.at[me], c_ss.at[k], c_rs.at[k], device_id={"ctx": to}, device_id_type=MESH
        )

    def row_copy(k):
        to = lax.rem(me + k, nctx)
        return pltpu.make_async_remote_copy(
            fsend.at[to], frecv.at[me], f_ss.at[k], f_rs.at[k], device_id={"ctx": to}, device_id_type=MESH
        )

    def lse_copy(k):
        to = lax.rem(me + k, nctx)
        return pltpu.make_async_remote_copy(
            lsend.at[to], lrecv.at[me], l_ss.at[k], l_rs.at[k], device_id={"ctx": to}, device_id_type=MESH
        )

    def each(count, act):
        def step(k, _):
            act(k)
            return 0

        lax.fori_loop(1, count, step, 0)

    r_out = lax.broadcasted_iota(jnp.int32, (rows, rows), 0)
    r_in = lax.broadcasted_iota(jnp.int32, (rows, rows), 1)
    per = rows // nhead
    order = jnp.where(r_in == lax.rem(r_out, per) * nhead + r_out // per, 1.0, 0.0).astype(BF16)
    qsend[...] = jnp.dot(order, queries[...], preferred_element_type=F32).astype(BF16).reshape(nhead, per, width)

    loads[0].wait()
    loads[1].wait()
    segment(0, 4)
    pl.semaphore_wait(barrier, nctx - 1 + nhead - 1)
    sibling(0).start()
    each(nhead, lambda k: query_copy(k).start())
    qrecv[head] = qsend[head]
    segment(1, 3)
    sibling(1).start()
    start_ring()
    segment(2, 5)
    sibling(2).start()

    used = owned // 128
    r = lax.broadcasted_iota(jnp.int32, (nctx * 8, 128), 0)
    pattern = jnp.where(lax.rem(r, 8) < used, (r // 8) * used + lax.rem(r, 8), -1)
    pattern = pattern.astype(F32).astype(BF16).reshape(nctx * 8 // 16, 16, 128)
    lanes = lax.broadcasted_iota(jnp.int32, (128, 128), 0).astype(F32).astype(BF16).reshape(8, 16, 128)
    rel[0] = lax.shift_right_logical(ids, 7).astype(F32)
    rel[1] = (ids & 127).astype(F32)
    part[0 : nctx * 8, 0:128] = jnp.zeros((nctx * 8, 128), F32)

    def count_step(n, _):
        both = []
        for side, table in ((0, pattern), (1, lanes)):
            block = rel[side, pl.ds(pl.multiple_of(n * (SEG // 128), 8), SEG // 128), :]
            pieces = []
            for u in range(SEG // 128):
                row = jnp.broadcast_to(block[u : u + 1, :], (16, 128)).astype(BF16)
                equal = table == row[None]
                pieces.append(jnp.where(equal, jnp.ones((), BF16), jnp.zeros((), BF16)).reshape(-1, 128))
            both.append(jnp.concatenate(pieces, axis=1))
        part[0 : nctx * 8, 0:128] += lax.dot_general(both[0], both[1], NT, preferred_element_type=F32)
        return 0

    lax.fori_loop(0, tokens // SEG, count_step, 0)
    csend[...] = part[0 : nctx * 8, 0:128].reshape(nctx, 8, 128)
    each(nctx, lambda k: count_copy(k).start())
    crecv[me] = csend[me]

    nblk = blocks.shape[1]
    lane = lax.broadcasted_iota(jnp.int32, (16, 128), 1)
    sub = lax.broadcasted_iota(jnp.int32, (16, 128), 0)
    spread = sub * 8 + lane // 16
    expanded = []
    for q in range(nblk // 128):
        source = jnp.broadcast_to(blocks[:, q * 128 : (q + 1) * 128], (16, 128))
        expanded.append(jnp.take_along_axis(source, spread, axis=1, mode="promise_in_bounds"))
    mine = me * owned + lax.broadcasted_iota(jnp.int32, (8, 128), 0) * 128
    mine = mine + lax.broadcasted_iota(jnp.int32, (8, 128), 1)
    dense = jnp.concatenate([ids] + expanded + [mine], axis=0)
    trows, crows = tokens // 128, cached // 128
    for s in range(steps):

        def hit(i, seen):
            return seen | (dense == sel[s, i]).astype(jnp.int32)

        seen = lax.fori_loop(0, sel.shape[1], hit, jnp.zeros(dense.shape, jnp.int32), unroll=8)
        hits[s, 0 : trows + crows, :] = jnp.where(seen[: trows + crows] > 0, 0.0, MASKED)
        hits[s, trows + crows :, :] = jnp.where(seen[trows + crows :] > 0, MASKED, 0.0)

    wide = TILE // 128
    copies = share // steps

    def spread_bias(n, _):
        for u in range(wide):
            per_step = [
                jnp.broadcast_to(hits[s, pl.ds(n * wide + u, 1), :], (copies, 128)) for s in range(steps)
            ]
            bias[n, :, u * 128 : (u + 1) * 128] = jnp.concatenate(per_step, axis=0)
        return 0

    lax.fori_loop(0, tiles, spread_bias, 0)

    forward(1, 0, 1)
    forward(2, 1, 1)

    segment(3, 2)
    sibling(3).start()
    segment(4, 6)
    sibling(4).start()

    each(nhead, lambda k: query_copy(k).wait_recv())
    q = qrecv[...].reshape(rows, width)
    factor = width**-0.5 * LOG2E
    mrun[...] = jnp.full(mrun.shape, FLOOR, F32)

    def score(n, _):
        keys = kv[pl.ds(pl.multiple_of(n * TILE, TILE), TILE), 0:width]
        raw = lax.dot_general(q, keys, NT, preferred_element_type=F32) * factor
        masked = (raw.reshape(nctx, share, TILE) + bias[n][None]).reshape(rows, TILE)
        scores[n] = masked
        top = masked[:, 0:128]
        for u in range(1, wide):
            top = jnp.maximum(top, masked[:, u * 128 : (u + 1) * 128])
        mrun[...] = jnp.maximum(mrun[...], top)
        return 0

    loads[2].wait()
    loads[3].wait()
    lax.fori_loop(0, tiles // 2, score, 0)

    forward(3, 0, 2)
    forward(4, 1, 2)
    segment(5, 1)
    sibling(5).start()
    segment(6, 7)
    sibling(6).start()
    lax.fori_loop(tiles // 2, tiles, score, 0)
    forward(5, 0, 3)
    forward(6, 1, 3)
    segment(7, 0)
    sibling(7).start()

    top_here = jnp.max(mrun[...], axis=1, keepdims=True)
    mrun[...] = jnp.broadcast_to(top_here, mrun.shape)
    lrun[...] = jnp.zeros_like(lrun)
    acc[...] = jnp.zeros_like(acc)

    def weigh(n, _):
        top = mrun[...]
        pieces, total = [], lrun[...]
        for u in range(wide):
            p = jnp.exp2(scores[n, :, u * 128 : (u + 1) * 128] - top)
            total = total + p
            pieces.append(p.astype(BF16))
        lrun[...] = total
        values = kv[pl.ds(pl.multiple_of(n * TILE, TILE), TILE), width : 2 * width]
        acc[...] += jnp.dot(jnp.concatenate(pieces, axis=1), values, preferred_element_type=F32)
        return 0

    lax.fori_loop(0, tiles, weigh, 0)
    total_here = jnp.sum(lrun[...], axis=1, keepdims=True)

    each(nctx, lambda k: count_copy(k).wait_recv())
    added = crecv[0]
    for k in range(1, nctx):
        added = added + crecv[k]
    added = added[0:used]
    before = old_counts[pl.ds(me * used, used), :]
    after = before + added
    diagonal = lax.broadcasted_iota(jnp.int32, (128, 128), 0) == lax.broadcasted_iota(jnp.int32, (128, 128), 1)

    def column(x):
        return jnp.concatenate(
            [jnp.sum(jnp.where(diagonal, x[u : u + 1, :], 0.0), axis=1, keepdims=True) for u in range(used)], axis=0
        )

    before_col, after_col = column(before), column(after)
    for u in range(used):
        out_n[:, u * 128 : (u + 1) * 128] = after[u : u + 1, :]
    log_counts = jnp.log(after) * LOG2E
    centre_bias = []
    for u in range(used):
        per_step = [
            jnp.broadcast_to(hits[s, trows + crows + u : trows + crows + u + 1, :], (copies, 128))
            for s in range(steps)
        ]
        centre_bias.append(jnp.concatenate(per_step, axis=0) + log_counts[u : u + 1, :])
    centre_bias = jnp.concatenate(centre_bias, axis=1)

    loads[4].wait()
    loads[5].wait()
    sibling(7).wait_recv()
    new = []
    for half, out in ((0, out_k), (1, out_v)):
        sums = mixed(7, half, [(0, 3), (1, 3)])
        value = (before_col * cen[half] + sums) / after_col
        out[...] = value
        new.append(value)

    k_high, k_mid, k_low = split3(new[0])
    raw = lax.dot_general(q, k_low, NT, preferred_element_type=F32)
    raw = raw + lax.dot_general(q, k_mid, NT, preferred_element_type=F32)
    raw = raw + lax.dot_general(q, k_high, NT, preferred_element_type=F32)
    centre = ((raw * factor).reshape(nctx, share, owned) + centre_bias[None]).reshape(rows, owned)
    top_centre = jnp.max(centre, axis=1, keepdims=True)
    top = jnp.maximum(top_here, top_centre)
    weights = jnp.exp2(centre - top)
    w_high, w_low = split2(weights)
    v_high, v_low = split2(new[1])
    gathered = jnp.dot(w_low, v_high, preferred_element_type=F32)
    gathered = gathered + jnp.dot(w_high, v_low, preferred_element_type=F32)
    gathered = gathered + jnp.dot(w_high, v_high, preferred_element_type=F32)
    rescale = jnp.exp2(top_here - top)
    whole = jnp.maximum(jnp.sum(weights, axis=1, keepdims=True) + rescale * total_here, 1e-30)
    result = (gathered + rescale * acc[...]) / whole
    lse = top + jnp.log(whole) * LOG2E

    fsend[...] = result.astype(BF16).reshape(nctx, share, width)
    spot = lax.broadcasted_iota(jnp.int32, (rows, 128), 1) == lax.rem(
        lax.broadcasted_iota(jnp.int32, (rows, 128), 0), share
    )
    by_owner = jnp.sum(jnp.where(spot, lse, 0.0).reshape(nctx, share, 128), axis=1)
    for k in range(nctx):
        lsend[k] = by_owner[k : k + 1, :]

    def send(k):
        lse_copy(k).start()
        row_copy(k).start()

    each(nctx, send)
    lrecv[me] = lsend[me]
    frecv[me] = fsend[me]

    each(nctx, lambda k: lse_copy(k).wait_recv())
    logs = jnp.concatenate([lrecv[k] for k in range(nctx)], axis=0)
    factors = jnp.exp2(logs - jnp.max(logs, axis=0, keepdims=True))
    factors = factors / jnp.sum(factors, axis=0, keepdims=True)
    by_row = jnp.transpose(jnp.concatenate([factors, jnp.zeros((128 - nctx, 128), F32)], axis=0))[0:share]
    each(nctx, lambda k: row_copy(k).wait_recv())
    final = jnp.zeros((share, width), F32)
    for k in range(nctx):
        final = final + by_row[:, k : k + 1] * frecv[k].astype(F32)
    out_a[...] = final.astype(BF16)

    for j in range(nz):
        sibling(j).wait_send()
    for copy in hops:
        copy.wait_send()
    each(nhead, lambda k: query_copy(k).wait_send())

    def sent(k):
        count_copy(k).wait_send()
        lse_copy(k).wait_send()
        row_copy(k).wait_send()

    each(nctx, sent)


def shards(
    stretch_keys,
    stretch_values,
    stretch_assign,
    centroid_keys,
    centroid_values,
    cluster_counts,
    cache_keys,
    cache_values,
    block_cluster,
    selected,
    queries,
):
    nctx, nhead = lax.axis_size("ctx"), lax.axis_size("head")
    clusters, width = centroid_keys.shape[1:]
    owned = clusters // nctx
    tokens, cached = stretch_keys.shape[1], cache_keys.shape[1]
    steps, qrows = queries.shape[:2]
    rows = steps * qrows * nhead
    share = rows // nctx
    nz = nctx // 2
    tiles = (tokens + cached) // TILE
    vmem = pl.BlockSpec(memory_space=pltpu.VMEM)
    smem = pl.BlockSpec(memory_space=pltpu.SMEM)
    hbm = pl.BlockSpec(memory_space=pl.ANY)
    dma = pltpu.SemaphoreType.DMA
    new_keys, new_values, new_counts, attended = pl.pallas_call(
        functools.partial(kernel, nctx, nhead, owned, steps, width),
        out_shape=(
            jax.ShapeDtypeStruct((owned, width), F32),
            jax.ShapeDtypeStruct((owned, width), F32),
            jax.ShapeDtypeStruct((1, owned), F32),
            jax.ShapeDtypeStruct((share, width), BF16),
        ),
        in_specs=[smem, vmem, vmem, vmem, vmem] + [hbm] * 6,
        out_specs=(vmem,) * 4,
        scratch_shapes=[
            pltpu.VMEM((tokens + cached, 2 * width), BF16),
            pltpu.VMEM((2, owned, width), F32),
            pltpu.VMEM((steps, (tokens + cached) // 128 + 8, 128), F32),
            pltpu.VMEM((tiles, share, TILE), F32),
            pltpu.VMEM((tiles, rows, TILE), F32),
            pltpu.VMEM((rows, 128), F32),
            pltpu.VMEM((rows, width), F32),
            pltpu.VMEM((rows, 128), F32),
            pltpu.VMEM((2, tokens // 128, 128), F32),
            pltpu.VMEM((2 * owned, 2 * width), F32),
            pltpu.VMEM((nz, owned, 2 * width), F32),
            pltpu.VMEM((nz, owned, 2 * width), BF16),
            pltpu.VMEM((nz, owned, 2 * width), BF16),
            pltpu.VMEM((16, owned, width), BF16),
            pltpu.VMEM((16, owned, width), BF16),
            pltpu.VMEM((nhead, rows // nhead, width), BF16),
            pltpu.VMEM((nhead, rows // nhead, width), BF16),
            pltpu.VMEM((nctx, 8, 128), F32),
            pltpu.VMEM((nctx, 8, 128), F32),
            pltpu.VMEM((nctx, share, width), BF16),
            pltpu.VMEM((nctx, share, width), BF16),
            pltpu.VMEM((nctx, 1, 128), F32),
            pltpu.VMEM((nctx, 1, 128), F32),
            dma((6,)),
            dma((nhead,)), dma((nhead,)), dma((nctx,)), dma((nctx,)), dma((nz,)), dma((nz,)),
            dma((16,)), dma((16,)), dma((nctx,)), dma((nctx,)), dma((nctx,)), dma((nctx,)),
        ],
        compiler_params=pltpu.CompilerParams(
            collective_id=0, has_side_effects=True, vmem_limit_bytes=50 * 1024 * 1024
        ),
        name="retrieve",
    )(
        selected.reshape(steps, selected.shape[2]),
        stretch_assign.reshape(tokens // 128, 128),
        block_cluster,
        cluster_counts.reshape(clusters // 128, 128),
        queries.reshape(rows, width),
        stretch_keys, stretch_values, cache_keys, cache_values, centroid_keys, centroid_values,
    )
    return (
        new_keys[None],
        new_values[None],
        new_counts,
        attended.reshape(steps, 1, share // steps, width),
    )


def solution(mesh):
    in_specs = (
        P("head", "ctx", None),
        P("head", "ctx", None),
        P("head", "ctx"),
        P("head", None, None),
        P("head", None, None),
        P("head", None),
        P("head", "ctx", None),
        P("head", "ctx", None),
        P("head", "ctx"),
        P(None, "head", None),
        P(None, "head", None, None),
    )
    out_specs = (
        P("head", "ctx", None),
        P("head", "ctx", None),
        P("head", "ctx"),
        P(None, "head", "ctx", None),
    )
    return jax.shard_map(shards, mesh=mesh, in_specs=in_specs, out_specs=out_specs, check_vma=False)
```

```python
import functools
import math

import jax
import jax.numpy as jnp
from jax import lax
from jax.experimental import pallas as pl
from jax.experimental.pallas import tpu as pltpu
from jax.sharding import PartitionSpec as P

MESH = pl.DeviceIdType.MESH
F32 = jnp.float32
BF16 = jnp.bfloat16
LOG2E = math.log2(math.e)
MASKED = -1e30
FLOOR = -1e29
TILE = 2048
NT = (((1,), (1,)), ((), ()))


def split2(x):
    high = x.astype(BF16)
    return high, (x - high.astype(F32)).astype(BF16)


def split3(x):
    high = x.astype(BF16)
    rest = x - high.astype(F32)
    mid = rest.astype(BF16)
    return high, mid, (rest - mid.astype(F32)).astype(BF16)


def kernel(
    nctx, nhead, owned, steps, width,
    sel_in, assign_in, blocks_in, counts_in, queries_in, skeys, svals, ckeys, cvals, cent_k, cent_v,
    out_k, out_v, out_n, out_a,
    sel, assign, blocks, old_counts, queries, kv, cen, hits, bias, scores, mrun, acc, lrun, rel, own,
    sib_send, sib_recv, ring_send, ring_recv, qsend, qrecv, csend, crecv, fsend, frecv, lsend, lrecv,
    load_sem, q_ss, q_rs, c_ss, c_rs, s_ss, s_rs, r_ss, r_rs, f_ss, f_rs, l_ss, l_rs,
):
    me = lax.axis_index("ctx")
    head = lax.axis_index("head")
    z, core = me // 2, lax.rem(me, 2)
    nz = nctx // 2
    tokens = skeys.shape[1]
    cached = ckeys.shape[1]
    rows = queries_in.shape[0]
    share = rows // nctx
    stretch_tiles = tokens // TILE
    tiles = (tokens + cached) // TILE

    loads = [
        pltpu.make_async_copy(skeys.at[0], kv.at[pl.ds(0, tokens), pl.ds(0, width)], load_sem.at[0]),
        pltpu.make_async_copy(svals.at[0], kv.at[pl.ds(0, tokens), pl.ds(width, width)], load_sem.at[1]),
        pltpu.make_async_copy(ckeys.at[0], kv.at[pl.ds(tokens, cached), pl.ds(0, width)], load_sem.at[2]),
        pltpu.make_async_copy(cvals.at[0], kv.at[pl.ds(tokens, cached), pl.ds(width, width)], load_sem.at[3]),
        pltpu.make_async_copy(cent_k.at[0, pl.ds(me * owned, owned), :], cen.at[0], load_sem.at[4]),
        pltpu.make_async_copy(cent_v.at[0, pl.ds(me * owned, owned), :], cen.at[1], load_sem.at[5]),
    ]
    small = [
        pltpu.make_async_copy(source, target, load_sem.at[6 + n])
        for n, (source, target) in enumerate(
            ((assign_in, assign), (queries_in, queries), (sel_in, sel), (blocks_in, blocks), (counts_in, old_counts))
        )
    ]
    small[0].start()
    loads[0].start()
    loads[1].start()
    for load in small[1:] + loads[2:]:
        load.start()

    barrier = pltpu.get_barrier_semaphore()

    def greet(k, _):
        pl.semaphore_signal(barrier, inc=1, device_id={"ctx": lax.rem(me + k, nctx)}, device_id_type=MESH)
        return 0

    def greet_heads(k, _):
        pl.semaphore_signal(barrier, inc=1, device_id={"head": lax.rem(head + k, nhead)}, device_id_type=MESH)
        return 0

    lax.fori_loop(1, nctx, greet, 0)
    lax.fori_loop(1, nhead, greet_heads, 0)

    small[0].wait()
    ids = assign[...]

    iota = lax.broadcasted_iota(jnp.int32, (owned, width), 0).astype(F32).astype(BF16)
    iota = iota.reshape(owned // 16, 16, width)

    def segment(j, offset):
        zd = lax.rem(z + offset, nz)
        rel[0] = (ids - owned * (2 * zd + 1 - core)).astype(F32)
        rel[1] = (ids - owned * (2 * zd + core)).astype(F32)
        hot = []
        for side in range(2):
            pieces = []
            for u in range(tokens // 128):
                row = jnp.broadcast_to(rel[side, u : u + 1, :], (16, 128)).astype(BF16)
                equal = iota == row[None]
                pieces.append(jnp.where(equal, jnp.ones((), BF16), jnp.zeros((), BF16)).reshape(owned, 128))
            hot.append(jnp.concatenate(pieces, axis=1))
        sums = jnp.dot(jnp.concatenate(hot, axis=0), kv[0:tokens, :], preferred_element_type=F32)
        sib_send[j] = sums[0:owned].astype(BF16)
        own[j] = sums[owned : 2 * owned]

    def sibling(j):
        return pltpu.make_async_remote_copy(
            sib_send.at[j], sib_recv.at[j], s_ss.at[j], s_rs.at[j],
            device_id={"ctx": 2 * z + 1 - core}, device_id_type=MESH,
        )

    def hop(direction, step, half):
        at = (direction * 4 + step) * 2 + half
        to = lax.rem(z + (1 if direction == 0 else nz - 1), nz)
        return pltpu.make_async_remote_copy(
            ring_send.at[at], ring_recv.at[at], r_ss.at[at], r_rs.at[at],
            device_id={"ctx": 2 * to + core}, device_id_type=MESH,
        )

    def mixed(j, half, arrivals):
        columns = slice(half * width, (half + 1) * width)
        value = own[j, :, columns] + sib_recv[j, :, columns].astype(F32)
        for direction, step in arrivals:
            hop(direction, step, half).wait_recv()
            value = value + ring_recv[(direction * 4 + step) * 2 + half].astype(F32)
        return value

    hops = []

    def forward(j, direction, step):
        sibling(j).wait_recv()
        first = 0 if direction == 0 else 1
        for half in (first, 1 - first):
            arrivals = []
            if step >= 2 or (step == 1 and half == first):
                arrivals = [(direction, step - 1)]
            ring_send[(direction * 4 + step) * 2 + half] = mixed(j, half, arrivals).astype(BF16)
            copy = hop(direction, step, half)
            copy.start()
            hops.append(copy)

    def start_ring():
        sibling(0).wait_recv()
        for direction in (0, 1):
            ring_send[direction * 8 + direction] = mixed(0, direction, []).astype(BF16)
            copy = hop(direction, 0, direction)
            copy.start()
            hops.append(copy)

    def query_copy(k):
        to = lax.rem(head + k, nhead)
        return pltpu.make_async_remote_copy(
            qsend.at[to], qrecv.at[head], q_ss.at[k], q_rs.at[k], device_id={"head": to}, device_id_type=MESH
        )

    def count_copy(k):
        to = lax.rem(me + k, nctx)
        return pltpu.make_async_remote_copy(
            csend.at[to], crecv.at[me], c_ss.at[k], c_rs.at[k], device_id={"ctx": to}, device_id_type=MESH
        )

    def row_copy(k):
        to = lax.rem(me + k, nctx)
        return pltpu.make_async_remote_copy(
            fsend.at[to], frecv.at[me], f_ss.at[k], f_rs.at[k], device_id={"ctx": to}, device_id_type=MESH
        )

    def lse_copy(k):
        to = lax.rem(me + k, nctx)
        return pltpu.make_async_remote_copy(
            lsend.at[to], lrecv.at[me], l_ss.at[k], l_rs.at[k], device_id={"ctx": to}, device_id_type=MESH
        )

    def each(count, act):
        def step(k, _):
            act(k)
            return 0

        lax.fori_loop(1, count, step, 0)

    r_out = lax.broadcasted_iota(jnp.int32, (rows, rows), 0)
    r_in = lax.broadcasted_iota(jnp.int32, (rows, rows), 1)
    per = rows // nhead
    order = jnp.where(r_in == lax.rem(r_out, per) * nhead + r_out // per, 1.0, 0.0).astype(BF16)
    small[1].wait()
    qsend[...] = jnp.dot(order, queries[...], preferred_element_type=F32).astype(BF16).reshape(nhead, per, width)

    loads[0].wait()
    loads[1].wait()
    segment(0, 4)
    pl.semaphore_wait(barrier, nctx - 1 + nhead - 1)
    sibling(0).start()
    each(nhead, lambda k: query_copy(k).start())
    qrecv[head] = qsend[head]
    segment(1, 3)
    sibling(1).start()
    start_ring()
    segment(2, 5)
    sibling(2).start()

    used = owned // 128
    r = lax.broadcasted_iota(jnp.int32, (nctx * 8, 128), 0)
    pattern = jnp.where(lax.rem(r, 8) < used, (r // 8) * used + lax.rem(r, 8), -1)
    pattern = pattern.astype(F32).astype(BF16).reshape(nctx * 8 // 16, 16, 128)
    lanes = lax.broadcasted_iota(jnp.int32, (128, 128), 0).astype(F32).astype(BF16).reshape(8, 16, 128)
    rel[0] = lax.shift_right_logical(ids, 7).astype(F32)
    rel[1] = (ids & 127).astype(F32)
    both = []
    for side, table in ((0, pattern), (1, lanes)):
        pieces = []
        for u in range(tokens // 128):
            row = jnp.broadcast_to(rel[side, u : u + 1, :], (16, 128)).astype(BF16)
            equal = table == row[None]
            pieces.append(jnp.where(equal, jnp.ones((), BF16), jnp.zeros((), BF16)).reshape(-1, 128))
        both.append(jnp.concatenate(pieces, axis=1))
    named = lax.dot_general(both[0], both[1], NT, preferred_element_type=F32)
    csend[...] = named.reshape(nctx, 8, 128)
    each(nctx, lambda k: count_copy(k).start())
    crecv[me] = csend[me]

    nblk = blocks.shape[1]
    small[2].wait()
    small[3].wait()
    small[4].wait()
    lane = lax.broadcasted_iota(jnp.int32, (16, 128), 1)
    sub = lax.broadcasted_iota(jnp.int32, (16, 128), 0)
    spread = sub * 8 + lane // 16
    expanded = []
    for q in range(nblk // 128):
        source = jnp.broadcast_to(blocks[:, q * 128 : (q + 1) * 128], (16, 128))
        expanded.append(jnp.take_along_axis(source, spread, axis=1, mode="promise_in_bounds"))
    mine = me * owned + lax.broadcasted_iota(jnp.int32, (8, 128), 0) * 128
    mine = mine + lax.broadcasted_iota(jnp.int32, (8, 128), 1)
    dense = jnp.concatenate([ids] + expanded + [mine], axis=0)
    trows, crows = tokens // 128, cached // 128
    for s in range(steps):

        def hit(i, seen):
            return seen | (dense == sel[s, i]).astype(jnp.int32)

        seen = lax.fori_loop(0, sel.shape[1], hit, jnp.zeros(dense.shape, jnp.int32), unroll=8)
        hits[s, 0 : trows + crows, :] = jnp.where(seen[: trows + crows] > 0, 0.0, MASKED)
        hits[s, trows + crows :, :] = jnp.where(seen[trows + crows :] > 0, MASKED, 0.0)

    wide = TILE // 128
    copies = share // steps

    def spread_bias(n, _):
        for u in range(wide):
            per_step = [
                jnp.broadcast_to(hits[s, pl.ds(n * wide + u, 1), :], (copies, 128)) for s in range(steps)
            ]
            bias[n, :, u * 128 : (u + 1) * 128] = jnp.concatenate(per_step, axis=0)
        return 0

    lax.fori_loop(0, tiles, spread_bias, 0)

    forward(1, 0, 1)
    forward(2, 1, 1)

    segment(3, 2)
    sibling(3).start()
    segment(4, 6)
    sibling(4).start()

    each(nhead, lambda k: query_copy(k).wait_recv())
    q = qrecv[...].reshape(rows, width)
    factor = width**-0.5 * LOG2E
    mrun[...] = jnp.full(mrun.shape, FLOOR, F32)

    def score(n, _):
        keys = kv[pl.ds(pl.multiple_of(n * TILE, TILE), TILE), 0:width]
        raw = lax.dot_general(q, keys, NT, preferred_element_type=F32) * factor
        masked = (raw.reshape(nctx, share, TILE) + bias[n][None]).reshape(rows, TILE)
        scores[n] = masked
        top = masked[:, 0:128]
        for u in range(1, wide):
            top = jnp.maximum(top, masked[:, u * 128 : (u + 1) * 128])
        mrun[...] = jnp.maximum(mrun[...], top)
        return 0

    loads[2].wait()
    loads[3].wait()
    lax.fori_loop(0, tiles // 2, score, 0)

    forward(3, 0, 2)
    forward(4, 1, 2)
    segment(5, 1)
    sibling(5).start()
    segment(6, 7)
    sibling(6).start()
    lax.fori_loop(tiles // 2, tiles, score, 0)
    forward(5, 0, 3)
    forward(6, 1, 3)
    segment(7, 0)
    sibling(7).start()

    top_here = jnp.max(mrun[...], axis=1, keepdims=True)
    mrun[...] = jnp.broadcast_to(top_here, mrun.shape)
    lrun[...] = jnp.zeros_like(lrun)
    acc[...] = jnp.zeros_like(acc)

    def weigh(n, _):
        top = mrun[...]
        pieces, total = [], lrun[...]
        for u in range(wide):
            p = jnp.exp2(scores[n, :, u * 128 : (u + 1) * 128] - top)
            total = total + p
            pieces.append(p.astype(BF16))
        lrun[...] = total
        values = kv[pl.ds(pl.multiple_of(n * TILE, TILE), TILE), width : 2 * width]
        acc[...] += jnp.dot(jnp.concatenate(pieces, axis=1), values, preferred_element_type=F32)
        return 0

    lax.fori_loop(0, tiles, weigh, 0)
    total_here = jnp.sum(lrun[...], axis=1, keepdims=True)

    each(nctx, lambda k: count_copy(k).wait_recv())
    added = crecv[0]
    for k in range(1, nctx):
        added = added + crecv[k]
    added = added[0:used]
    before = old_counts[pl.ds(me * used, used), :]
    after = before + added
    diagonal = lax.broadcasted_iota(jnp.int32, (128, 128), 0) == lax.broadcasted_iota(jnp.int32, (128, 128), 1)

    def column(x):
        return jnp.concatenate(
            [jnp.sum(jnp.where(diagonal, x[u : u + 1, :], 0.0), axis=1, keepdims=True) for u in range(used)], axis=0
        )

    before_col, after_col = column(before), column(after)
    for u in range(used):
        out_n[:, u * 128 : (u + 1) * 128] = after[u : u + 1, :]
    log_counts = jnp.log(after) * LOG2E
    centre_bias = []
    for u in range(used):
        per_step = [
            jnp.broadcast_to(hits[s, trows + crows + u : trows + crows + u + 1, :], (copies, 128))
            for s in range(steps)
        ]
        centre_bias.append(jnp.concatenate(per_step, axis=0) + log_counts[u : u + 1, :])
    centre_bias = jnp.concatenate(centre_bias, axis=1)

    loads[4].wait()
    loads[5].wait()
    sibling(7).wait_recv()
    new = []
    for half, out in ((0, out_k), (1, out_v)):
        sums = mixed(7, half, [(0, 3), (1, 3)])
        value = (before_col * cen[half] + sums) / after_col
        out[...] = value
        new.append(value)

    k_high, k_mid, k_low = split3(new[0])
    raw = lax.dot_general(q, k_low, NT, preferred_element_type=F32)
    raw = raw + lax.dot_general(q, k_mid, NT, preferred_element_type=F32)
    raw = raw + lax.dot_general(q, k_high, NT, preferred_element_type=F32)
    centre = ((raw * factor).reshape(nctx, share, owned) + centre_bias[None]).reshape(rows, owned)
    top_centre = jnp.max(centre, axis=1, keepdims=True)
    top = jnp.maximum(top_here, top_centre)
    weights = jnp.exp2(centre - top)
    w_high, w_low = split2(weights)
    v_high, v_low = split2(new[1])
    gathered = jnp.dot(w_low, v_high, preferred_element_type=F32)
    gathered = gathered + jnp.dot(w_high, v_low, preferred_element_type=F32)
    gathered = gathered + jnp.dot(w_high, v_high, preferred_element_type=F32)
    rescale = jnp.exp2(top_here - top)
    whole = jnp.maximum(jnp.sum(weights, axis=1, keepdims=True) + rescale * total_here, 1e-30)
    result = (gathered + rescale * acc[...]) / whole
    lse = top + jnp.log(whole) * LOG2E

    fsend[...] = result.astype(BF16).reshape(nctx, share, width)
    spot = lax.broadcasted_iota(jnp.int32, (rows, 128), 1) == lax.rem(
        lax.broadcasted_iota(jnp.int32, (rows, 128), 0), share
    )
    by_owner = jnp.sum(jnp.where(spot, lse, 0.0).reshape(nctx, share, 128), axis=1)
    for k in range(nctx):
        lsend[k] = by_owner[k : k + 1, :]

    def send(k):
        lse_copy(k).start()
        row_copy(k).start()

    each(nctx, send)
    lrecv[me] = lsend[me]
    frecv[me] = fsend[me]

    each(nctx, lambda k: lse_copy(k).wait_recv())
    logs = jnp.concatenate([lrecv[k] for k in range(nctx)], axis=0)
    factors = jnp.exp2(logs - jnp.max(logs, axis=0, keepdims=True))
    factors = factors / jnp.sum(factors, axis=0, keepdims=True)
    by_row = jnp.transpose(jnp.concatenate([factors, jnp.zeros((128 - nctx, 128), F32)], axis=0))[0:share]
    each(nctx, lambda k: row_copy(k).wait_recv())
    final = jnp.zeros((share, width), F32)
    for k in range(nctx):
        final = final + by_row[:, k : k + 1] * frecv[k].astype(F32)
    out_a[...] = final.astype(BF16)

    for j in range(nz):
        sibling(j).wait_send()
    for copy in hops:
        copy.wait_send()
    each(nhead, lambda k: query_copy(k).wait_send())

    def sent(k):
        count_copy(k).wait_send()
        lse_copy(k).wait_send()
        row_copy(k).wait_send()

    each(nctx, sent)


def shards(
    stretch_keys,
    stretch_values,
    stretch_assign,
    centroid_keys,
    centroid_values,
    cluster_counts,
    cache_keys,
    cache_values,
    block_cluster,
    selected,
    queries,
):
    nctx, nhead = lax.axis_size("ctx"), lax.axis_size("head")
    clusters, width = centroid_keys.shape[1:]
    owned = clusters // nctx
    tokens, cached = stretch_keys.shape[1], cache_keys.shape[1]
    steps, qrows = queries.shape[:2]
    rows = steps * qrows * nhead
    share = rows // nctx
    nz = nctx // 2
    tiles = (tokens + cached) // TILE
    vmem = pl.BlockSpec(memory_space=pltpu.VMEM)
    hbm = pl.BlockSpec(memory_space=pltpu.HBM)
    dma = pltpu.SemaphoreType.DMA
    new_keys, new_values, new_counts, attended = pl.pallas_call(
        functools.partial(kernel, nctx, nhead, owned, steps, width),
        out_shape=(
            jax.ShapeDtypeStruct((owned, width), F32),
            jax.ShapeDtypeStruct((owned, width), F32),
            jax.ShapeDtypeStruct((1, owned), F32),
            jax.ShapeDtypeStruct((share, width), BF16),
        ),
        in_specs=[hbm] * 11,
        out_specs=(vmem,) * 4,
        scratch_shapes=[
            pltpu.SMEM((steps, selected.shape[2]), jnp.int32),
            pltpu.VMEM((tokens // 128, 128), jnp.int32),
            pltpu.VMEM(block_cluster.shape, jnp.int32),
            pltpu.VMEM((clusters // 128, 128), F32),
            pltpu.VMEM((rows, width), BF16),
            pltpu.VMEM((tokens + cached, 2 * width), BF16),
            pltpu.VMEM((2, owned, width), F32),
            pltpu.VMEM((steps, (tokens + cached) // 128 + 8, 128), F32),
            pltpu.VMEM((tiles, share, TILE), F32),
            pltpu.VMEM((tiles, rows, TILE), F32),
            pltpu.VMEM((rows, 128), F32),
            pltpu.VMEM((rows, width), F32),
            pltpu.VMEM((rows, 128), F32),
            pltpu.VMEM((2, tokens // 128, 128), F32),
            pltpu.VMEM((nz, owned, 2 * width), F32),
            pltpu.VMEM((nz, owned, 2 * width), BF16),
            pltpu.VMEM((nz, owned, 2 * width), BF16),
            pltpu.VMEM((16, owned, width), BF16),
            pltpu.VMEM((16, owned, width), BF16),
            pltpu.VMEM((nhead, rows // nhead, width), BF16),
            pltpu.VMEM((nhead, rows // nhead, width), BF16),
            pltpu.VMEM((nctx, 8, 128), F32),
            pltpu.VMEM((nctx, 8, 128), F32),
            pltpu.VMEM((nctx, share, width), BF16),
            pltpu.VMEM((nctx, share, width), BF16),
            pltpu.VMEM((nctx, 1, 128), F32),
            pltpu.VMEM((nctx, 1, 128), F32),
            dma((11,)),
            dma((nhead,)), dma((nhead,)), dma((nctx,)), dma((nctx,)), dma((nz,)), dma((nz,)),
            dma((16,)), dma((16,)), dma((nctx,)), dma((nctx,)), dma((nctx,)), dma((nctx,)),
        ],
        compiler_params=pltpu.CompilerParams(
            collective_id=0, has_side_effects=True, vmem_limit_bytes=60000000
        ),
        name="retrieve",
    )(
        selected.reshape(steps, selected.shape[2]),
        stretch_assign.reshape(tokens // 128, 128),
        block_cluster,
        cluster_counts.reshape(clusters // 128, 128),
        queries.reshape(rows, width),
        stretch_keys, stretch_values, cache_keys, cache_values, centroid_keys, centroid_values,
    )
    return (
        new_keys[None],
        new_values[None],
        new_counts,
        attended.reshape(steps, 1, share // steps, width),
    )


def solution(mesh):
    in_specs = (
        P("head", "ctx", None),
        P("head", "ctx", None),
        P("head", "ctx"),
        P("head", None, None),
        P("head", None, None),
        P("head", None),
        P("head", "ctx", None),
        P("head", "ctx", None),
        P("head", "ctx"),
        P(None, "head", None),
        P(None, "head", None, None),
    )
    out_specs = (
        P("head", "ctx", None),
        P("head", "ctx", None),
        P("head", "ctx"),
        P(None, "head", "ctx", None),
    )
    return jax.shard_map(shards, mesh=mesh, in_specs=in_specs, out_specs=out_specs, check_vma=False)
```

```python
import functools
import math

import jax
import jax.numpy as jnp
from jax import lax
from jax.experimental import pallas as pl
from jax.experimental.pallas import tpu as pltpu
from jax.sharding import PartitionSpec as P

MESH = pl.DeviceIdType.MESH
F32 = jnp.float32
BF16 = jnp.bfloat16
LOG2E = math.log2(math.e)
MASKED = -1e30
FLOOR = -1e29
TILE = 2048
NT = (((1,), (1,)), ((), ()))


def split2(x):
    high = x.astype(BF16)
    return high, (x - high.astype(F32)).astype(BF16)


def split3(x):
    high = x.astype(BF16)
    rest = x - high.astype(F32)
    mid = rest.astype(BF16)
    return high, mid, (rest - mid.astype(F32)).astype(BF16)


def kernel(
    nctx, nhead, owned, steps, width,
    sel_in, assign_in, blocks_in, counts_in, queries_in, skeys, svals, ckeys, cvals, cent_k, cent_v,
    out_k, out_v, out_n, out_a,
    sel, assign, blocks, old_counts, queries, kv, cen, hits, bias, scores, mrun, acc, lrun, rel, own,
    sib_send, sib_recv, ring_send, ring_recv, qsend, qrecv, named, fsend, frecv,
    load_sem, q_ss, q_rs, s_ss, s_rs, r_ss, r_rs, f_ss, f_rs,
):
    me = lax.axis_index("ctx")
    head = lax.axis_index("head")
    z, core = me // 2, lax.rem(me, 2)
    nz = nctx // 2
    tokens = skeys.shape[1]
    cached = ckeys.shape[1]
    rows = queries_in.shape[0]
    share = rows // nctx
    stretch_tiles = tokens // TILE
    tiles = (tokens + cached) // TILE

    loads = [
        pltpu.make_async_copy(skeys.at[0], kv.at[pl.ds(0, tokens), pl.ds(0, width)], load_sem.at[0]),
        pltpu.make_async_copy(svals.at[0], kv.at[pl.ds(0, tokens), pl.ds(width, width)], load_sem.at[1]),
        pltpu.make_async_copy(ckeys.at[0], kv.at[pl.ds(tokens, cached), pl.ds(0, width)], load_sem.at[2]),
        pltpu.make_async_copy(cvals.at[0], kv.at[pl.ds(tokens, cached), pl.ds(width, width)], load_sem.at[3]),
        pltpu.make_async_copy(cent_k.at[0, pl.ds(me * owned, owned), :], cen.at[0], load_sem.at[4]),
        pltpu.make_async_copy(cent_v.at[0, pl.ds(me * owned, owned), :], cen.at[1], load_sem.at[5]),
    ]
    small = [
        pltpu.make_async_copy(source, target, load_sem.at[6 + n])
        for n, (source, target) in enumerate(
            ((assign_in, assign), (queries_in, queries), (sel_in, sel), (blocks_in, blocks), (counts_in, old_counts))
        )
    ]
    small[0].start()
    loads[0].start()
    loads[1].start()
    for load in small[1:] + loads[2:]:
        load.start()

    barrier = pltpu.get_barrier_semaphore()

    def greet(k, _):
        pl.semaphore_signal(barrier, inc=1, device_id={"ctx": lax.rem(me + k, nctx)}, device_id_type=MESH)
        return 0

    def greet_heads(k, _):
        pl.semaphore_signal(barrier, inc=1, device_id={"head": lax.rem(head + k, nhead)}, device_id_type=MESH)
        return 0

    lax.fori_loop(1, nctx, greet, 0)
    lax.fori_loop(1, nhead, greet_heads, 0)

    small[0].wait()
    ids = assign[...]

    iota = lax.broadcasted_iota(jnp.int32, (owned, width), 0).astype(F32).astype(BF16)
    iota = iota.reshape(owned // 16, 16, width)

    def counts_out(value):
        high = jnp.floor(value * (1 / 256))
        return jnp.concatenate([value - 256 * high, high], axis=0).astype(BF16)

    def counts_in(tile):
        tile = tile.astype(F32)
        return tile[0:8] + 256 * tile[8:16]

    def segment(j, offset):
        zd = lax.rem(z + offset, nz)
        rel[0] = (ids - owned * (2 * zd + 1 - core)).astype(F32)
        rel[1] = (ids - owned * (2 * zd + core)).astype(F32)
        hot = []
        for side in range(2):
            pieces = []
            for u in range(tokens // 128):
                row = jnp.broadcast_to(rel[side, u : u + 1, :], (16, 128)).astype(BF16)
                equal = iota == row[None]
                pieces.append(jnp.where(equal, jnp.ones((), BF16), jnp.zeros((), BF16)).reshape(owned, 128))
            hot.append(jnp.concatenate(pieces, axis=1))
        sums = jnp.dot(jnp.concatenate(hot, axis=0), kv[0:tokens, :], preferred_element_type=F32)
        sib_send[j, 0:owned, :] = sums[0:owned].astype(BF16)
        sib_send[j, owned:, 0:width] = counts_out(named[2 * zd + 1 - core])
        sib_send[j, owned:, width:] = jnp.zeros((16, width), BF16)
        own[j] = sums[owned : 2 * owned]
        if j == 0:
            pl.semaphore_wait(barrier, nctx - 1 + nhead - 1)
        sibling(j).start()

    def sibling(j):
        return pltpu.make_async_remote_copy(
            sib_send.at[j], sib_recv.at[j], s_ss.at[j], s_rs.at[j],
            device_id={"ctx": 2 * z + 1 - core}, device_id_type=MESH,
        )

    def hop(direction, step, half):
        at = (direction * 4 + step) * 2 + half
        to = lax.rem(z + (1 if direction == 0 else nz - 1), nz)
        length = owned + (16 if half == 0 else 0)
        return pltpu.make_async_remote_copy(
            ring_send.at[at, pl.ds(0, length), :], ring_recv.at[at, pl.ds(0, length), :], r_ss.at[at], r_rs.at[at],
            device_id={"ctx": 2 * to + core}, device_id_type=MESH,
        )

    def mixed(j, offset, half, arrivals):
        columns = slice(half * width, (half + 1) * width)
        value = own[j, :, columns] + sib_recv[j, 0:owned, columns].astype(F32)
        count = None
        if half == 0:
            count = named[2 * lax.rem(z + offset, nz) + core] + counts_in(sib_recv[j, owned:, 0:width])
        for direction, step in arrivals:
            hop(direction, step, half).wait_recv()
            at = (direction * 4 + step) * 2 + half
            value = value + ring_recv[at, 0:owned, :].astype(F32)
            if half == 0:
                count = count + counts_in(ring_recv[at, owned:, :])
        return value, count

    hops = []

    def launch(j, offset, direction, step, half, arrivals):
        at = (direction * 4 + step) * 2 + half
        value, count = mixed(j, offset, half, arrivals)
        ring_send[at, 0:owned, :] = value.astype(BF16)
        if half == 0:
            ring_send[at, owned:, :] = counts_out(count)
        copy = hop(direction, step, half)
        copy.start()
        hops.append(copy)

    def forward(j, offset, direction, step):
        sibling(j).wait_recv()
        first = 0 if direction == 0 else 1
        for half in (first, 1 - first):
            arrivals = []
            if step >= 2 or (step == 1 and half == first):
                arrivals = [(direction, step - 1)]
            launch(j, offset, direction, step, half, arrivals)

    def start_ring():
        sibling(0).wait_recv()
        for direction in (0, 1):
            launch(0, 4, direction, 0, direction, [])

    def query_copy(k):
        to = lax.rem(head + k, nhead)
        return pltpu.make_async_remote_copy(
            qsend.at[to], qrecv.at[head], q_ss, q_rs, device_id={"head": to}, device_id_type=MESH
        )

    def row_copy(k):
        to = lax.rem(me + k, nctx)
        return pltpu.make_async_remote_copy(
            fsend.at[to], frecv.at[me], f_ss, f_rs, device_id={"ctx": to}, device_id_type=MESH
        )

    def all_queries():
        part = pl.ds(0, nhead - 1)
        return pltpu.make_async_remote_copy(
            qsend.at[part], qrecv.at[part], q_ss, q_rs, device_id={"head": lax.rem(head + 1, nhead)}, device_id_type=MESH
        )

    def all_rows():
        part = pl.ds(0, nctx - 1)
        return pltpu.make_async_remote_copy(
            fsend.at[part], frecv.at[part], f_ss, f_rs, device_id={"ctx": lax.rem(me + 1, nctx)}, device_id_type=MESH
        )

    def each(count, act):
        def step(k, _):
            act(k)
            return 0

        lax.fori_loop(1, count, step, 0)

    used = owned // 128
    r = lax.broadcasted_iota(jnp.int32, (nctx * 8, 128), 0)
    pattern = jnp.where(lax.rem(r, 8) < used, (r // 8) * used + lax.rem(r, 8), -1)
    pattern = pattern.astype(F32).astype(BF16).reshape(nctx * 8 // 16, 16, 128)
    lanes = lax.broadcasted_iota(jnp.int32, (128, 128), 0).astype(F32).astype(BF16).reshape(8, 16, 128)
    rel[0] = lax.shift_right_logical(ids, 7).astype(F32)
    rel[1] = (ids & 127).astype(F32)
    both = []
    for side, table in ((0, pattern), (1, lanes)):
        pieces = []
        for u in range(tokens // 128):
            row = jnp.broadcast_to(rel[side, u : u + 1, :], (16, 128)).astype(BF16)
            equal = table == row[None]
            pieces.append(jnp.where(equal, jnp.ones((), BF16), jnp.zeros((), BF16)).reshape(-1, 128))
        both.append(jnp.concatenate(pieces, axis=1))
    tally = lax.dot_general(both[0], both[1], NT, preferred_element_type=F32)
    named[...] = tally.reshape(nctx, 8, 128)

    r_out = lax.broadcasted_iota(jnp.int32, (rows, rows), 0)
    r_in = lax.broadcasted_iota(jnp.int32, (rows, rows), 1)
    per = rows // nhead
    order = jnp.where(r_in == lax.rem(r_out, per) * nhead + r_out // per, 1.0, 0.0).astype(BF16)
    small[1].wait()
    qsend[...] = jnp.dot(order, queries[...], preferred_element_type=F32).astype(BF16).reshape(nhead, per, width)

    loads[0].wait()
    loads[1].wait()
    segment(0, 4)
    each(nhead, lambda k: query_copy(k).start())
    qrecv[head] = qsend[head]
    segment(1, 3)
    start_ring()
    segment(2, 5)

    nblk = blocks.shape[1]
    small[2].wait()
    small[3].wait()
    small[4].wait()
    lane = lax.broadcasted_iota(jnp.int32, (16, 128), 1)
    sub = lax.broadcasted_iota(jnp.int32, (16, 128), 0)
    spread = sub * 8 + lane // 16
    expanded = []
    for q in range(nblk // 128):
        source = jnp.broadcast_to(blocks[:, q * 128 : (q + 1) * 128], (16, 128))
        expanded.append(jnp.take_along_axis(source, spread, axis=1, mode="promise_in_bounds"))
    mine = me * owned + lax.broadcasted_iota(jnp.int32, (8, 128), 0) * 128
    mine = mine + lax.broadcasted_iota(jnp.int32, (8, 128), 1)
    dense = jnp.concatenate([ids] + expanded + [mine], axis=0)
    trows, crows = tokens // 128, cached // 128
    for s in range(steps):

        def hit(i, seen):
            return seen | (dense == sel[s, i]).astype(jnp.int32)

        seen = lax.fori_loop(0, sel.shape[1], hit, jnp.zeros(dense.shape, jnp.int32), unroll=8)
        hits[s, 0 : trows + crows, :] = jnp.where(seen[: trows + crows] > 0, 0.0, MASKED)
        hits[s, trows + crows :, :] = jnp.where(seen[trows + crows :] > 0, MASKED, 0.0)

    wide = TILE // 128
    copies = share // steps

    def spread_bias(n, _):
        for u in range(wide):
            per_step = [
                jnp.broadcast_to(hits[s, pl.ds(n * wide + u, 1), :], (copies, 128)) for s in range(steps)
            ]
            bias[n, :, u * 128 : (u + 1) * 128] = jnp.concatenate(per_step, axis=0)
        return 0

    lax.fori_loop(0, tiles, spread_bias, 0)

    forward(1, 3, 0, 1)
    forward(2, 5, 1, 1)

    segment(3, 2)
    segment(4, 6)

    all_queries().wait_recv()
    q = qrecv[...].reshape(rows, width)
    factor = width**-0.5 * LOG2E
    mrun[...] = jnp.full(mrun.shape, FLOOR, F32)

    def score(n, _):
        keys = kv[pl.ds(pl.multiple_of(n * TILE, TILE), TILE), 0:width]
        raw = lax.dot_general(q, keys, NT, preferred_element_type=F32) * factor
        masked = (raw.reshape(nctx, share, TILE) + bias[n][None]).reshape(rows, TILE)
        scores[n] = masked
        top = masked[:, 0:128]
        for u in range(1, wide):
            top = jnp.maximum(top, masked[:, u * 128 : (u + 1) * 128])
        mrun[...] = jnp.maximum(mrun[...], top)
        return 0

    loads[2].wait()
    loads[3].wait()
    lax.fori_loop(0, tiles // 2, score, 0)

    forward(3, 2, 0, 2)
    forward(4, 6, 1, 2)
    segment(5, 1)
    segment(6, 7)
    lax.fori_loop(tiles // 2, tiles, score, 0)
    forward(5, 1, 0, 3)
    forward(6, 7, 1, 3)
    segment(7, 0)

    top_here = jnp.max(mrun[...], axis=1, keepdims=True)
    mrun[...] = jnp.broadcast_to(top_here, mrun.shape)
    lrun[...] = jnp.zeros_like(lrun)
    acc[...] = jnp.zeros_like(acc)

    def weigh(n, _):
        top = mrun[...]
        pieces, total = [], lrun[...]
        for u in range(wide):
            p = jnp.exp2(scores[n, :, u * 128 : (u + 1) * 128] - top)
            total = total + p
            pieces.append(p.astype(BF16))
        lrun[...] = total
        values = kv[pl.ds(pl.multiple_of(n * TILE, TILE), TILE), width : 2 * width]
        acc[...] += jnp.dot(jnp.concatenate(pieces, axis=1), values, preferred_element_type=F32)
        return 0

    lax.fori_loop(0, tiles, weigh, 0)
    total_here = jnp.sum(lrun[...], axis=1, keepdims=True)

    loads[4].wait()
    loads[5].wait()
    sibling(7).wait_recv()
    ends = [(0, 3), (1, 3)]
    key_sums, added = mixed(7, 0, 0, ends)
    value_sums, _ = mixed(7, 0, 1, ends)
    added = added[0:used]
    before = old_counts[pl.ds(me * used, used), :]
    after = before + added
    diagonal = lax.broadcasted_iota(jnp.int32, (128, 128), 0) == lax.broadcasted_iota(jnp.int32, (128, 128), 1)

    def column(x):
        return jnp.concatenate(
            [jnp.sum(jnp.where(diagonal, x[u : u + 1, :], 0.0), axis=1, keepdims=True) for u in range(used)], axis=0
        )

    before_col, after_col = column(before), column(after)
    for u in range(used):
        out_n[:, u * 128 : (u + 1) * 128] = after[u : u + 1, :]
    log_counts = jnp.log(after) * LOG2E
    centre_bias = []
    for u in range(used):
        per_step = [
            jnp.broadcast_to(hits[s, trows + crows + u : trows + crows + u + 1, :], (copies, 128))
            for s in range(steps)
        ]
        centre_bias.append(jnp.concatenate(per_step, axis=0) + log_counts[u : u + 1, :])
    centre_bias = jnp.concatenate(centre_bias, axis=1)

    new = []
    for half, out, sums in ((0, out_k, key_sums), (1, out_v, value_sums)):
        value = (before_col * cen[half] + sums) / after_col
        out[...] = value
        new.append(value)

    k_high, k_mid, k_low = split3(new[0])
    raw = lax.dot_general(q, k_low, NT, preferred_element_type=F32)
    raw = raw + lax.dot_general(q, k_mid, NT, preferred_element_type=F32)
    raw = raw + lax.dot_general(q, k_high, NT, preferred_element_type=F32)
    centre = ((raw * factor).reshape(nctx, share, owned) + centre_bias[None]).reshape(rows, owned)
    top_centre = jnp.max(centre, axis=1, keepdims=True)
    top = jnp.maximum(top_here, top_centre)
    weights = jnp.exp2(centre - top)
    w_high, w_low = split2(weights)
    v_high, v_low = split2(new[1])
    gathered = jnp.dot(w_low, v_high, preferred_element_type=F32)
    gathered = gathered + jnp.dot(w_high, v_low, preferred_element_type=F32)
    gathered = gathered + jnp.dot(w_high, v_high, preferred_element_type=F32)
    rescale = jnp.exp2(top_here - top)
    whole = jnp.maximum(jnp.sum(weights, axis=1, keepdims=True) + rescale * total_here, 1e-30)
    result = (gathered + rescale * acc[...]) / whole
    lse = top + jnp.log(whole) * LOG2E

    fsend[:, 0:share, :] = result.astype(BF16).reshape(nctx, share, width)
    spot = lax.broadcasted_iota(jnp.int32, (rows, 128), 1)
    high, mid, low = (x.astype(F32) for x in split3(lse))
    three = jnp.where(spot == 0, high, jnp.where(spot == 1, mid, jnp.where(spot == 2, low, 0.0)))
    fsend[:, share:, :] = three.astype(BF16).reshape(nctx, share, 128)
    each(nctx, lambda k: row_copy(k).start())
    frecv[me] = fsend[me]
    for copy in hops:
        copy.wait_send()
    for j in range(nz):
        sibling(j).wait_send()
    all_queries().wait_send()
    all_rows().wait_recv()
    logs = jnp.sum(frecv[:, share:, :].astype(F32), axis=2, keepdims=True)
    factors = jnp.exp2(logs - jnp.max(logs, axis=0, keepdims=True))
    final = jnp.sum(factors * frecv[:, 0:share, :].astype(F32), axis=0) / jnp.sum(factors, axis=0)
    out_a[...] = final.astype(BF16)
    all_rows().wait_send()


def finish_kernel(k_in, v_in, n_in, a_in, k_out, v_out, n_out, a_out):
    for source, target in ((k_in, k_out), (v_in, v_out), (n_in, n_out), (a_in, a_out)):
        target[...] = source[...]


def shards(
    stretch_keys,
    stretch_values,
    stretch_assign,
    centroid_keys,
    centroid_values,
    cluster_counts,
    cache_keys,
    cache_values,
    block_cluster,
    selected,
    queries,
):
    nctx, nhead = lax.axis_size("ctx"), lax.axis_size("head")
    clusters, width = centroid_keys.shape[1:]
    owned = clusters // nctx
    tokens, cached = stretch_keys.shape[1], cache_keys.shape[1]
    steps, qrows = queries.shape[:2]
    rows = steps * qrows * nhead
    share = rows // nctx
    nz = nctx // 2
    tiles = (tokens + cached) // TILE
    vmem = pl.BlockSpec(memory_space=pltpu.VMEM)
    hbm = pl.BlockSpec(memory_space=pltpu.HBM)
    dma = pltpu.SemaphoreType.DMA
    shapes = (
        jax.ShapeDtypeStruct((owned, width), F32),
        jax.ShapeDtypeStruct((owned, width), F32),
        jax.ShapeDtypeStruct((1, owned), F32),
        jax.ShapeDtypeStruct((share, width), BF16),
    )
    results = pl.pallas_call(
        functools.partial(kernel, nctx, nhead, owned, steps, width),
        out_shape=shapes,
        in_specs=[hbm] * 11,
        out_specs=(vmem,) * 4,
        scratch_shapes=[
            pltpu.SMEM((steps, selected.shape[2]), jnp.int32),
            pltpu.VMEM((tokens // 128, 128), jnp.int32),
            pltpu.VMEM(block_cluster.shape, jnp.int32),
            pltpu.VMEM((clusters // 128, 128), F32),
            pltpu.VMEM((rows, width), BF16),
            pltpu.VMEM((tokens + cached, 2 * width), BF16),
            pltpu.VMEM((2, owned, width), F32),
            pltpu.VMEM((steps, (tokens + cached) // 128 + 8, 128), F32),
            pltpu.VMEM((tiles, share, TILE), F32),
            pltpu.VMEM((tiles, rows, TILE), F32),
            pltpu.VMEM((rows, 128), F32),
            pltpu.VMEM((rows, width), F32),
            pltpu.VMEM((rows, 128), F32),
            pltpu.VMEM((2, tokens // 128, 128), F32),
            pltpu.VMEM((nz, owned, 2 * width), F32),
            pltpu.VMEM((nz, owned + 16, 2 * width), BF16),
            pltpu.VMEM((nz, owned + 16, 2 * width), BF16),
            pltpu.VMEM((16, owned + 16, width), BF16),
            pltpu.VMEM((16, owned + 16, width), BF16),
            pltpu.VMEM((nhead, rows // nhead, width), BF16),
            pltpu.VMEM((nhead, rows // nhead, width), BF16),
            pltpu.VMEM((nctx, 8, 128), F32),
            pltpu.VMEM((nctx, 2 * share, width), BF16),
            pltpu.VMEM((nctx, 2 * share, width), BF16),
            dma((11,)),
            dma(()), dma(()), dma((nz,)), dma((nz,)), dma((16,)), dma((16,)), dma(()), dma(()),
        ],
        compiler_params=pltpu.CompilerParams(
            collective_id=0, has_side_effects=True, vmem_limit_bytes=60000000
        ),
        name="retrieve",
    )(
        selected.reshape(steps, selected.shape[2]),
        stretch_assign.reshape(tokens // 128, 128),
        block_cluster,
        cluster_counts.reshape(clusters // 128, 128),
        queries.reshape(rows, width),
        stretch_keys, stretch_values, cache_keys, cache_values, centroid_keys, centroid_values,
    )
    new_keys, new_values, new_counts, attended = pl.pallas_call(
        finish_kernel,
        out_shape=shapes,
        in_specs=[vmem] * 4,
        out_specs=(vmem,) * 4,
        name="finish",
    )(*results)
    return (
        new_keys[None],
        new_values[None],
        new_counts,
        attended.reshape(steps, 1, share // steps, width),
    )


def solution(mesh):
    in_specs = (
        P("head", "ctx", None),
        P("head", "ctx", None),
        P("head", "ctx"),
        P("head", None, None),
        P("head", None, None),
        P("head", None),
        P("head", "ctx", None),
        P("head", "ctx", None),
        P("head", "ctx"),
        P(None, "head", None),
        P(None, "head", None, None),
    )
    out_specs = (
        P("head", "ctx", None),
        P("head", "ctx", None),
        P("head", "ctx"),
        P(None, "head", "ctx", None),
    )
    return jax.shard_map(shards, mesh=mesh, in_specs=in_specs, out_specs=out_specs, check_vma=False)
```

```python
import functools
import math

import jax
import jax.numpy as jnp
from jax import lax
from jax.experimental import pallas as pl
from jax.experimental.pallas import tpu as pltpu
from jax.sharding import PartitionSpec as P

MESH = pl.DeviceIdType.MESH
F32 = jnp.float32
BF16 = jnp.bfloat16
LOG2E = math.log2(math.e)
MASKED = -1e30
FLOOR = -1e29
TILE = 2048
NT = (((1,), (1,)), ((), ()))


def split2(x):
    high = x.astype(BF16)
    return high, (x - high.astype(F32)).astype(BF16)


def split3(x):
    high = x.astype(BF16)
    rest = x - high.astype(F32)
    mid = rest.astype(BF16)
    return high, mid, (rest - mid.astype(F32)).astype(BF16)


def kernel(
    nctx, nhead, owned, steps, width,
    sel_in, assign_in, blocks_in, counts_in, queries_in, skeys, svals, ckeys, cvals, cent_k, cent_v,
    out_k, out_v, out_n, out_a,
    sel, assign, blocks, old_counts, queries, kv, cen, member, bias, scores, mrun, acc, lrun, rel, own,
    sib_send, sib_recv, ring_send, ring_recv, qsend, qrecv, named, fsend, frecv,
    load_sem, q_ss, q_rs, s_ss, s_rs, r_ss, r_rs, f_ss, f_rs,
):
    me = lax.axis_index("ctx")
    head = lax.axis_index("head")
    z, core = me // 2, lax.rem(me, 2)
    nz = nctx // 2
    tokens = skeys.shape[1]
    cached = ckeys.shape[1]
    rows = queries_in.shape[0]
    share = rows // nctx
    stretch_tiles = tokens // TILE
    tiles = (tokens + cached) // TILE

    loads = [
        pltpu.make_async_copy(skeys.at[0], kv.at[pl.ds(0, tokens), pl.ds(0, width)], load_sem.at[0]),
        pltpu.make_async_copy(svals.at[0], kv.at[pl.ds(0, tokens), pl.ds(width, width)], load_sem.at[1]),
        pltpu.make_async_copy(ckeys.at[0], kv.at[pl.ds(tokens, cached), pl.ds(0, width)], load_sem.at[2]),
        pltpu.make_async_copy(cvals.at[0], kv.at[pl.ds(tokens, cached), pl.ds(width, width)], load_sem.at[3]),
        pltpu.make_async_copy(cent_k.at[0, pl.ds(me * owned, owned), :], cen.at[0], load_sem.at[4]),
        pltpu.make_async_copy(cent_v.at[0, pl.ds(me * owned, owned), :], cen.at[1], load_sem.at[5]),
    ]
    small = [
        pltpu.make_async_copy(source, target, load_sem.at[6 + n])
        for n, (source, target) in enumerate(
            ((assign_in, assign), (queries_in, queries), (sel_in, sel), (blocks_in, blocks), (counts_in, old_counts))
        )
    ]
    small[0].start()
    loads[0].start()
    loads[1].start()
    for load in small[1:] + loads[2:]:
        load.start()

    barrier = pltpu.get_barrier_semaphore()

    def greet(k, _):
        pl.semaphore_signal(barrier, inc=1, device_id={"ctx": lax.rem(me + k, nctx)}, device_id_type=MESH)
        return 0

    def greet_heads(k, _):
        pl.semaphore_signal(barrier, inc=1, device_id={"head": lax.rem(head + k, nhead)}, device_id_type=MESH)
        return 0

    lax.fori_loop(1, nctx, greet, 0)
    lax.fori_loop(1, nhead, greet_heads, 0)

    small[0].wait()
    ids = assign[...]

    iota = lax.broadcasted_iota(jnp.int32, (owned, width), 0).astype(F32).astype(BF16)
    iota = iota.reshape(owned // 16, 16, width)

    def counts_out(value):
        high = jnp.floor(value * (1 / 256))
        return jnp.concatenate([value - 256 * high, high], axis=0).astype(BF16)

    def counts_in(tile):
        tile = tile.astype(F32)
        return tile[0:8] + 256 * tile[8:16]

    def segment(j, offset):
        zd = lax.rem(z + offset, nz)
        rel[0] = (ids - owned * (2 * zd + 1 - core)).astype(F32)
        rel[1] = (ids - owned * (2 * zd + core)).astype(F32)
        hot = []
        for side in range(2):
            pieces = []
            for u in range(tokens // 128):
                row = jnp.broadcast_to(rel[side, u : u + 1, :], (16, 128)).astype(BF16)
                equal = iota == row[None]
                pieces.append(jnp.where(equal, jnp.ones((), BF16), jnp.zeros((), BF16)).reshape(owned, 128))
            hot.append(jnp.concatenate(pieces, axis=1))
        sums = jnp.dot(jnp.concatenate(hot, axis=0), kv[0:tokens, :], preferred_element_type=F32)
        sib_send[j, 0:owned, :] = sums[0:owned].astype(BF16)
        sib_send[j, owned:, 0:width] = counts_out(named[2 * zd + 1 - core])
        sib_send[j, owned:, width:] = jnp.zeros((16, width), BF16)
        own[j] = sums[owned : 2 * owned]
        if j == 0:
            pl.semaphore_wait(barrier, nctx - 1 + nhead - 1)
        sibling(j).start()

    def sibling(j):
        return pltpu.make_async_remote_copy(
            sib_send.at[j], sib_recv.at[j], s_ss.at[j], s_rs.at[j],
            device_id={"ctx": 2 * z + 1 - core}, device_id_type=MESH,
        )

    def hop(direction, step, half):
        at = (direction * 4 + step) * 2 + half
        to = lax.rem(z + (1 if direction == 0 else nz - 1), nz)
        length = owned + (16 if half == 0 else 0)
        return pltpu.make_async_remote_copy(
            ring_send.at[at, pl.ds(0, length), :], ring_recv.at[at, pl.ds(0, length), :], r_ss.at[at], r_rs.at[at],
            device_id={"ctx": 2 * to + core}, device_id_type=MESH,
        )

    def mixed(j, offset, half, arrivals):
        columns = slice(half * width, (half + 1) * width)
        value = own[j, :, columns] + sib_recv[j, 0:owned, columns].astype(F32)
        count = None
        if half == 0:
            count = named[2 * lax.rem(z + offset, nz) + core] + counts_in(sib_recv[j, owned:, 0:width])
        for direction, step in arrivals:
            hop(direction, step, half).wait_recv()
            at = (direction * 4 + step) * 2 + half
            value = value + ring_recv[at, 0:owned, :].astype(F32)
            if half == 0:
                count = count + counts_in(ring_recv[at, owned:, :])
        return value, count

    hops = []

    def launch(j, offset, direction, step, half, arrivals):
        at = (direction * 4 + step) * 2 + half
        value, count = mixed(j, offset, half, arrivals)
        ring_send[at, 0:owned, :] = value.astype(BF16)
        if half == 0:
            ring_send[at, owned:, :] = counts_out(count)
        copy = hop(direction, step, half)
        copy.start()
        hops.append(copy)

    def forward(j, offset, direction, step):
        sibling(j).wait_recv()
        first = 0 if direction == 0 else 1
        for half in (first, 1 - first):
            arrivals = []
            if step >= 2 or (step == 1 and half == first):
                arrivals = [(direction, step - 1)]
            launch(j, offset, direction, step, half, arrivals)

    def start_ring():
        sibling(0).wait_recv()
        for direction in (0, 1):
            launch(0, 4, direction, 0, direction, [])

    def query_copy(k):
        to = lax.rem(head + k, nhead)
        return pltpu.make_async_remote_copy(
            qsend.at[to], qrecv.at[head], q_ss, q_rs, device_id={"head": to}, device_id_type=MESH
        )

    def row_copy(k):
        to = lax.rem(me + k, nctx)
        return pltpu.make_async_remote_copy(
            fsend.at[to], frecv.at[me], f_ss, f_rs, device_id={"ctx": to}, device_id_type=MESH
        )

    def all_queries():
        part = pl.ds(0, nhead - 1)
        return pltpu.make_async_remote_copy(
            qsend.at[part], qrecv.at[part], q_ss, q_rs, device_id={"head": lax.rem(head + 1, nhead)}, device_id_type=MESH
        )

    def all_rows():
        part = pl.ds(0, nctx - 1)
        return pltpu.make_async_remote_copy(
            fsend.at[part], frecv.at[part], f_ss, f_rs, device_id={"ctx": lax.rem(me + 1, nctx)}, device_id_type=MESH
        )

    def each(count, act):
        def step(k, _):
            act(k)
            return 0

        lax.fori_loop(1, count, step, 0)

    used = owned // 128
    high_rows = nctx * used
    pattern = lax.broadcasted_iota(jnp.int32, (high_rows, 128), 0).astype(F32).astype(BF16)
    pattern = pattern.reshape(high_rows // 16, 16, 128)
    lanes = lax.broadcasted_iota(jnp.int32, (128, 128), 0).astype(F32).astype(BF16).reshape(8, 16, 128)
    rel[0] = lax.shift_right_logical(ids, 7).astype(F32)
    rel[1] = (ids & 127).astype(F32)
    both = []
    for side, table in ((0, pattern), (1, lanes)):
        pieces = []
        for u in range(tokens // 128):
            row = jnp.broadcast_to(rel[side, u : u + 1, :], (16, 128)).astype(BF16)
            equal = table == row[None]
            pieces.append(jnp.where(equal, jnp.ones((), BF16), jnp.zeros((), BF16)).reshape(-1, 128))
        both.append(jnp.concatenate(pieces, axis=1))
    tally = lax.dot_general(both[0], both[1], NT, preferred_element_type=F32)
    named[...] = jnp.zeros_like(named)
    for k in range(nctx):
        named[k, 0:used, :] = tally[k * used : (k + 1) * used]

    r_out = lax.broadcasted_iota(jnp.int32, (rows, rows), 0)
    r_in = lax.broadcasted_iota(jnp.int32, (rows, rows), 1)
    per = rows // nhead
    order = jnp.where(r_in == lax.rem(r_out, per) * nhead + r_out // per, 1.0, 0.0).astype(BF16)
    small[1].wait()
    qsend[...] = jnp.dot(order, queries[...], preferred_element_type=F32).astype(BF16).reshape(nhead, per, width)

    loads[0].wait()
    loads[1].wait()
    segment(0, 4)
    each(nhead, lambda k: query_copy(k).start())
    qrecv[head] = qsend[head]
    segment(1, 3)
    start_ring()
    segment(2, 5)

    small[2].wait()
    small[3].wait()
    small[4].wait()
    picks = sel.shape[1]
    hi_rows = lax.broadcasted_iota(jnp.int32, (high_rows, picks), 0)
    lo_rows = lax.broadcasted_iota(jnp.int32, (128, picks), 0)
    bits = jnp.zeros((high_rows, 128), jnp.int32)
    for s in range(steps):
        chosen = sel[s : s + 1, :]
        hi_hot = (hi_rows == lax.shift_right_logical(chosen, 7)).astype(F32).astype(BF16)
        lo_hot = (lo_rows == (chosen & 127)).astype(F32).astype(BF16)
        found = lax.dot_general(hi_hot, lo_hot, NT, preferred_element_type=F32)
        bits = bits + jnp.where(found > 0.5, 1 << s, 0)
    member[...] = bits

    nblk = blocks.shape[1]
    lane = lax.broadcasted_iota(jnp.int32, (16, 128), 1)
    sub = lax.broadcasted_iota(jnp.int32, (16, 128), 0)
    spread = sub * 8 + lane // 16
    expanded = []
    for q in range(nblk // 128):
        source = jnp.broadcast_to(blocks[:, q * 128 : (q + 1) * 128], (16, 128))
        expanded.append(jnp.take_along_axis(source, spread, axis=1, mode="promise_in_bounds"))
    dense = jnp.concatenate([ids] + expanded, axis=0)
    hi, lo = lax.shift_right_logical(dense, 7), dense & 127
    seen = jnp.zeros(dense.shape, jnp.int32)
    for r in range(high_rows):
        row = jnp.broadcast_to(bits[r : r + 1, :], dense.shape)
        seen = jnp.where(hi == r, jnp.take_along_axis(row, lo, axis=1, mode="promise_in_bounds"), seen)
    wide = TILE // 128
    mask_of = lax.shift_left(jnp.ones((share, 128), jnp.int32), sub // (share // steps))
    for n in range(tiles):
        for u in range(wide):
            picked = jnp.broadcast_to(seen[n * wide + u : n * wide + u + 1, :], (share, 128)) & mask_of
            bias[n, :, u * 128 : (u + 1) * 128] = jnp.where(picked != 0, 0.0, MASKED)

    forward(1, 3, 0, 1)
    forward(2, 5, 1, 1)

    segment(3, 2)
    segment(4, 6)

    all_queries().wait_recv()
    q = qrecv[...].reshape(rows, width)
    factor = width**-0.5 * LOG2E
    mrun[...] = jnp.full(mrun.shape, FLOOR, F32)

    def score(n, _):
        keys = kv[pl.ds(pl.multiple_of(n * TILE, TILE), TILE), 0:width]
        raw = lax.dot_general(q, keys, NT, preferred_element_type=F32) * factor
        masked = (raw.reshape(nctx, share, TILE) + bias[n][None]).reshape(rows, TILE)
        scores[n] = masked
        top = masked[:, 0:128]
        for u in range(1, wide):
            top = jnp.maximum(top, masked[:, u * 128 : (u + 1) * 128])
        mrun[...] = jnp.maximum(mrun[...], top)
        return 0

    loads[2].wait()
    loads[3].wait()
    lax.fori_loop(0, tiles // 2, score, 0)

    forward(3, 2, 0, 2)
    forward(4, 6, 1, 2)
    segment(5, 1)
    segment(6, 7)
    lax.fori_loop(tiles // 2, tiles, score, 0)
    forward(5, 1, 0, 3)
    forward(6, 7, 1, 3)
    segment(7, 0)

    top_here = jnp.max(mrun[...], axis=1, keepdims=True)
    mrun[...] = jnp.broadcast_to(top_here, mrun.shape)
    lrun[...] = jnp.zeros_like(lrun)
    acc[...] = jnp.zeros_like(acc)

    def weigh(n, _):
        top = mrun[...]
        pieces, total = [], lrun[...]
        for u in range(wide):
            p = jnp.exp2(scores[n, :, u * 128 : (u + 1) * 128] - top)
            total = total + p
            pieces.append(p.astype(BF16))
        lrun[...] = total
        values = kv[pl.ds(pl.multiple_of(n * TILE, TILE), TILE), width : 2 * width]
        acc[...] += jnp.dot(jnp.concatenate(pieces, axis=1), values, preferred_element_type=F32)
        return 0

    lax.fori_loop(0, tiles, weigh, 0)
    total_here = jnp.sum(lrun[...], axis=1, keepdims=True)

    loads[4].wait()
    loads[5].wait()
    sibling(7).wait_recv()
    ends = [(0, 3), (1, 3)]
    key_sums, added = mixed(7, 0, 0, ends)
    value_sums, _ = mixed(7, 0, 1, ends)
    added = added[0:used]
    before = old_counts[pl.ds(me * used, used), :]
    after = before + added
    diagonal = lax.broadcasted_iota(jnp.int32, (128, 128), 0) == lax.broadcasted_iota(jnp.int32, (128, 128), 1)

    def column(x):
        return jnp.concatenate(
            [jnp.sum(jnp.where(diagonal, x[u : u + 1, :], 0.0), axis=1, keepdims=True) for u in range(used)], axis=0
        )

    before_col, after_col = column(before), column(after)
    for u in range(used):
        out_n[:, u * 128 : (u + 1) * 128] = after[u : u + 1, :]
    log_counts = jnp.log(after) * LOG2E
    centre_bias = []
    own_bits = member[pl.ds(me * used, used), :]
    for u in range(used):
        picked = jnp.broadcast_to(own_bits[u : u + 1, :], (share, 128)) & mask_of
        centre_bias.append(jnp.where(picked != 0, MASKED, 0.0) + log_counts[u : u + 1, :])
    centre_bias = jnp.concatenate(centre_bias, axis=1)

    new = []
    for half, out, sums in ((0, out_k, key_sums), (1, out_v, value_sums)):
        value = (before_col * cen[half] + sums) / after_col
        out[...] = value
        new.append(value)

    k_high, k_mid, k_low = split3(new[0])
    raw = lax.dot_general(q, k_low, NT, preferred_element_type=F32)
    raw = raw + lax.dot_general(q, k_mid, NT, preferred_element_type=F32)
    raw = raw + lax.dot_general(q, k_high, NT, preferred_element_type=F32)
    centre = ((raw * factor).reshape(nctx, share, owned) + centre_bias[None]).reshape(rows, owned)
    top_centre = jnp.max(centre, axis=1, keepdims=True)
    top = jnp.maximum(top_here, top_centre)
    weights = jnp.exp2(centre - top)
    w_high, w_low = split2(weights)
    v_high, v_low = split2(new[1])
    gathered = jnp.dot(w_low, v_high, preferred_element_type=F32)
    gathered = gathered + jnp.dot(w_high, v_low, preferred_element_type=F32)
    gathered = gathered + jnp.dot(w_high, v_high, preferred_element_type=F32)
    rescale = jnp.exp2(top_here - top)
    whole = jnp.maximum(jnp.sum(weights, axis=1, keepdims=True) + rescale * total_here, 1e-30)
    result = (gathered + rescale * acc[...]) / whole
    lse = top + jnp.log(whole) * LOG2E

    fsend[:, 0:share, :] = result.astype(BF16).reshape(nctx, share, width)
    spot = lax.broadcasted_iota(jnp.int32, (rows, 128), 1)
    high, mid, low = (x.astype(F32) for x in split3(lse))
    three = jnp.where(spot == 0, high, jnp.where(spot == 1, mid, jnp.where(spot == 2, low, 0.0)))
    fsend[:, share:, :] = three.astype(BF16).reshape(nctx, share, 128)
    half = nctx // 2
    row_copy(half).start()
    for k in range(1, half):
        row_copy(half - k).start()
        row_copy(half + k).start()
    frecv[me] = fsend[me]
    for copy in hops:
        copy.wait_send()
    for j in range(nz):
        sibling(j).wait_send()
    all_queries().wait_send()
    all_rows().wait_recv()
    logs = jnp.sum(frecv[:, share:, :].astype(F32), axis=2, keepdims=True)
    factors = jnp.exp2(logs - jnp.max(logs, axis=0, keepdims=True))
    final = jnp.sum(factors * frecv[:, 0:share, :].astype(F32), axis=0) / jnp.sum(factors, axis=0)
    out_a[...] = final.astype(BF16)
    all_rows().wait_send()


def finish_kernel(k_in, v_in, n_in, a_in, k_out, v_out, n_out, a_out):
    for source, target in ((k_in, k_out), (v_in, v_out), (n_in, n_out), (a_in, a_out)):
        target[...] = source[...]


def shards(
    stretch_keys,
    stretch_values,
    stretch_assign,
    centroid_keys,
    centroid_values,
    cluster_counts,
    cache_keys,
    cache_values,
    block_cluster,
    selected,
    queries,
):
    nctx, nhead = lax.axis_size("ctx"), lax.axis_size("head")
    clusters, width = centroid_keys.shape[1:]
    owned = clusters // nctx
    tokens, cached = stretch_keys.shape[1], cache_keys.shape[1]
    steps, qrows = queries.shape[:2]
    rows = steps * qrows * nhead
    share = rows // nctx
    nz = nctx // 2
    tiles = (tokens + cached) // TILE
    vmem = pl.BlockSpec(memory_space=pltpu.VMEM)
    hbm = pl.BlockSpec(memory_space=pltpu.HBM)
    dma = pltpu.SemaphoreType.DMA
    shapes = (
        jax.ShapeDtypeStruct((owned, width), F32),
        jax.ShapeDtypeStruct((owned, width), F32),
        jax.ShapeDtypeStruct((1, owned), F32),
        jax.ShapeDtypeStruct((share, width), BF16),
    )
    results = pl.pallas_call(
        functools.partial(kernel, nctx, nhead, owned, steps, width),
        out_shape=shapes,
        in_specs=[hbm] * 11,
        out_specs=(vmem,) * 4,
        scratch_shapes=[
            pltpu.VMEM((steps, selected.shape[2]), jnp.int32),
            pltpu.VMEM((tokens // 128, 128), jnp.int32),
            pltpu.VMEM(block_cluster.shape, jnp.int32),
            pltpu.VMEM((clusters // 128, 128), F32),
            pltpu.VMEM((rows, width), BF16),
            pltpu.VMEM((tokens + cached, 2 * width), BF16),
            pltpu.VMEM((2, owned, width), F32),
            pltpu.VMEM((clusters // 128, 128), jnp.int32),
            pltpu.VMEM((tiles, share, TILE), F32),
            pltpu.VMEM((tiles, rows, TILE), F32),
            pltpu.VMEM((rows, 128), F32),
            pltpu.VMEM((rows, width), F32),
            pltpu.VMEM((rows, 128), F32),
            pltpu.VMEM((2, tokens // 128, 128), F32),
            pltpu.VMEM((nz, owned, 2 * width), F32),
            pltpu.VMEM((nz, owned + 16, 2 * width), BF16),
            pltpu.VMEM((nz, owned + 16, 2 * width), BF16),
            pltpu.VMEM((16, owned + 16, width), BF16),
            pltpu.VMEM((16, owned + 16, width), BF16),
            pltpu.VMEM((nhead, rows // nhead, width), BF16),
            pltpu.VMEM((nhead, rows // nhead, width), BF16),
            pltpu.VMEM((nctx, 8, 128), F32),
            pltpu.VMEM((nctx, 2 * share, width), BF16),
            pltpu.VMEM((nctx, 2 * share, width), BF16),
            dma((11,)),
            dma(()), dma(()), dma((nz,)), dma((nz,)), dma((16,)), dma((16,)), dma(()), dma(()),
        ],
        compiler_params=pltpu.CompilerParams(
            collective_id=0, has_side_effects=True, vmem_limit_bytes=60000000
        ),
        name="retrieve",
    )(
        selected.reshape(steps, selected.shape[2]),
        stretch_assign.reshape(tokens // 128, 128),
        block_cluster,
        cluster_counts.reshape(clusters // 128, 128),
        queries.reshape(rows, width),
        stretch_keys, stretch_values, cache_keys, cache_values, centroid_keys, centroid_values,
    )
    new_keys, new_values, new_counts, attended = pl.pallas_call(
        finish_kernel,
        out_shape=shapes,
        in_specs=[vmem] * 4,
        out_specs=(vmem,) * 4,
        name="finish",
    )(*results)
    return (
        new_keys[None],
        new_values[None],
        new_counts,
        attended.reshape(steps, 1, share // steps, width),
    )


def solution(mesh):
    in_specs = (
        P("head", "ctx", None),
        P("head", "ctx", None),
        P("head", "ctx"),
        P("head", None, None),
        P("head", None, None),
        P("head", None),
        P("head", "ctx", None),
        P("head", "ctx", None),
        P("head", "ctx"),
        P(None, "head", None),
        P(None, "head", None, None),
    )
    out_specs = (
        P("head", "ctx", None),
        P("head", "ctx", None),
        P("head", "ctx"),
        P(None, "head", "ctx", None),
    )
    return jax.shard_map(shards, mesh=mesh, in_specs=in_specs, out_specs=out_specs, check_vma=False)
```

```python
import functools
import math

import jax
import jax.numpy as jnp
from jax import lax
from jax.experimental import pallas as pl
from jax.experimental.pallas import tpu as pltpu
from jax.sharding import PartitionSpec as P

MESH = pl.DeviceIdType.MESH
F32 = jnp.float32
BF16 = jnp.bfloat16
LOG2E = math.log2(math.e)
MASKED = -1e30
FLOOR = -1e29
TILE = 3072
NT = (((1,), (1,)), ((), ()))


def split2(x):
    high = x.astype(BF16)
    return high, (x - high.astype(F32)).astype(BF16)


def split3(x):
    high = x.astype(BF16)
    rest = x - high.astype(F32)
    mid = rest.astype(BF16)
    return high, mid, (rest - mid.astype(F32)).astype(BF16)


def kernel(
    nctx, nhead, owned, steps, width,
    sel_in, assign_in, blocks_in, counts_in, queries_in, skeys, svals, ckeys, cvals, cent_k, cent_v,
    out_k, out_v, out_n, out_a,
    sel, assign, blocks, old_counts, queries, kv, cen, member, bias, scores, mrun, acc, lrun, rel, own,
    sib_send, sib_recv, ring_send, ring_recv, qsend, qrecv, named, fsend, frecv,
    load_sem, q_ss, q_rs, s_ss, s_rs, r_ss, r_rs, f_ss, f_rs,
):
    me = lax.axis_index("ctx")
    head = lax.axis_index("head")
    z, core = me // 2, lax.rem(me, 2)
    nz = nctx // 2
    tokens = skeys.shape[1]
    cached = ckeys.shape[1]
    rows = queries_in.shape[0]
    share = rows // nctx
    stretch_tiles = tokens // TILE
    tiles = (tokens + cached) // TILE

    loads = [
        pltpu.make_async_copy(skeys.at[0], kv.at[pl.ds(0, tokens), pl.ds(0, width)], load_sem.at[0]),
        pltpu.make_async_copy(svals.at[0], kv.at[pl.ds(0, tokens), pl.ds(width, width)], load_sem.at[1]),
        pltpu.make_async_copy(ckeys.at[0], kv.at[pl.ds(tokens, cached), pl.ds(0, width)], load_sem.at[2]),
        pltpu.make_async_copy(cvals.at[0], kv.at[pl.ds(tokens, cached), pl.ds(width, width)], load_sem.at[3]),
        pltpu.make_async_copy(cent_k.at[0, pl.ds(me * owned, owned), :], cen.at[0], load_sem.at[4]),
        pltpu.make_async_copy(cent_v.at[0, pl.ds(me * owned, owned), :], cen.at[1], load_sem.at[5]),
    ]
    small = [
        pltpu.make_async_copy(source, target, load_sem.at[6 + n])
        for n, (source, target) in enumerate(
            ((assign_in, assign), (queries_in, queries), (sel_in, sel), (blocks_in, blocks), (counts_in, old_counts))
        )
    ]
    small[0].start()
    loads[0].start()
    loads[1].start()
    for load in small[1:] + loads[2:]:
        load.start()

    barrier = pltpu.get_barrier_semaphore()

    def greet(k, _):
        pl.semaphore_signal(barrier, inc=1, device_id={"ctx": lax.rem(me + k, nctx)}, device_id_type=MESH)
        return 0

    def greet_heads(k, _):
        pl.semaphore_signal(barrier, inc=1, device_id={"head": lax.rem(head + k, nhead)}, device_id_type=MESH)
        return 0

    lax.fori_loop(1, nctx, greet, 0)
    lax.fori_loop(1, nhead, greet_heads, 0)

    small[0].wait()
    ids = assign[...]

    iota = lax.broadcasted_iota(jnp.int32, (owned, width), 0).astype(F32).astype(BF16)
    iota = iota.reshape(owned // 16, 16, width)

    def counts_out(value):
        high = jnp.floor(value * (1 / 256))
        return jnp.concatenate([value - 256 * high, high], axis=0).astype(BF16)

    def counts_in(tile):
        tile = tile.astype(F32)
        return tile[0:8] + 256 * tile[8:16]

    def segment(j, offset):
        zd = lax.rem(z + offset, nz)
        rel[0] = (ids - owned * (2 * zd + 1 - core)).astype(F32)
        rel[1] = (ids - owned * (2 * zd + core)).astype(F32)
        hot = []
        for side in range(2):
            pieces = []
            for u in range(tokens // 128):
                row = jnp.broadcast_to(rel[side, u : u + 1, :], (16, 128)).astype(BF16)
                equal = iota == row[None]
                pieces.append(jnp.where(equal, jnp.ones((), BF16), jnp.zeros((), BF16)).reshape(owned, 128))
            hot.append(jnp.concatenate(pieces, axis=1))
        sums = jnp.dot(jnp.concatenate(hot, axis=0), kv[0:tokens, :], preferred_element_type=F32)
        sib_send[j, 0:owned, :] = sums[0:owned].astype(BF16)
        sib_send[j, owned:, 0:width] = counts_out(named[2 * zd + 1 - core])
        sib_send[j, owned:, width:] = jnp.zeros((16, width), BF16)
        own[j] = sums[owned : 2 * owned]

    def sibling(j):
        return pltpu.make_async_remote_copy(
            sib_send.at[j], sib_recv.at[j], s_ss.at[j], s_rs.at[j],
            device_id={"ctx": 2 * z + 1 - core}, device_id_type=MESH,
        )

    def hop(direction, step, half):
        at = (direction * 4 + step) * 2 + half
        to = lax.rem(z + (1 if direction == 0 else nz - 1), nz)
        length = owned + (16 if half == 0 else 0)
        return pltpu.make_async_remote_copy(
            ring_send.at[at, pl.ds(0, length), :], ring_recv.at[at, pl.ds(0, length), :], r_ss.at[at], r_rs.at[at],
            device_id={"ctx": 2 * to + core}, device_id_type=MESH,
        )

    def mixed(j, offset, half, arrivals):
        columns = slice(half * width, (half + 1) * width)
        value = own[j, :, columns] + sib_recv[j, 0:owned, columns].astype(F32)
        count = None
        if half == 0:
            count = named[2 * lax.rem(z + offset, nz) + core] + counts_in(sib_recv[j, owned:, 0:width])
        for direction, step in arrivals:
            hop(direction, step, half).wait_recv()
            at = (direction * 4 + step) * 2 + half
            value = value + ring_recv[at, 0:owned, :].astype(F32)
            if half == 0:
                count = count + counts_in(ring_recv[at, owned:, :])
        return value, count

    hops = []

    def launch(j, offset, direction, step, half, arrivals):
        at = (direction * 4 + step) * 2 + half
        value, count = mixed(j, offset, half, arrivals)
        ring_send[at, 0:owned, :] = value.astype(BF16)
        if half == 0:
            ring_send[at, owned:, :] = counts_out(count)
        copy = hop(direction, step, half)
        copy.start()
        hops.append(copy)

    def forward(j, offset, direction, step):
        sibling(j).wait_recv()
        first = 0 if direction == 0 else 1
        for half in (first, 1 - first):
            arrivals = []
            if step >= 2 or (step == 1 and half == first):
                arrivals = [(direction, step - 1)]
            launch(j, offset, direction, step, half, arrivals)

    def start_ring():
        sibling(0).wait_recv()
        for direction in (0, 1):
            launch(0, 4, direction, 0, direction, [])

    def query_copy(k):
        to = lax.rem(head + k, nhead)
        return pltpu.make_async_remote_copy(
            qsend.at[to], qrecv.at[head], q_ss, q_rs, device_id={"head": to}, device_id_type=MESH
        )

    def row_copy(k):
        to = lax.rem(me + k, nctx)
        return pltpu.make_async_remote_copy(
            fsend.at[to], frecv.at[me], f_ss, f_rs, device_id={"ctx": to}, device_id_type=MESH
        )

    def all_queries():
        part = pl.ds(0, nhead - 1)
        return pltpu.make_async_remote_copy(
            qsend.at[part], qrecv.at[part], q_ss, q_rs, device_id={"head": lax.rem(head + 1, nhead)}, device_id_type=MESH
        )

    def all_rows():
        part = pl.ds(0, nctx - 1)
        return pltpu.make_async_remote_copy(
            fsend.at[part], frecv.at[part], f_ss, f_rs, device_id={"ctx": lax.rem(me + 1, nctx)}, device_id_type=MESH
        )

    def each(count, act):
        def step(k, _):
            act(k)
            return 0

        lax.fori_loop(1, count, step, 0)

    used = owned // 128
    high_rows = nctx * used
    pattern = lax.broadcasted_iota(jnp.int32, (high_rows, 128), 0).astype(F32).astype(BF16)
    pattern = pattern.reshape(high_rows // 16, 16, 128)
    lanes = lax.broadcasted_iota(jnp.int32, (128, 128), 0).astype(F32).astype(BF16).reshape(8, 16, 128)
    rel[0] = lax.shift_right_logical(ids, 7).astype(F32)
    rel[1] = (ids & 127).astype(F32)
    both = []
    for side, table in ((0, pattern), (1, lanes)):
        pieces = []
        for u in range(tokens // 128):
            row = jnp.broadcast_to(rel[side, u : u + 1, :], (16, 128)).astype(BF16)
            equal = table == row[None]
            pieces.append(jnp.where(equal, jnp.ones((), BF16), jnp.zeros((), BF16)).reshape(-1, 128))
        both.append(jnp.concatenate(pieces, axis=1))
    tally = lax.dot_general(both[0], both[1], NT, preferred_element_type=F32)
    named[...] = jnp.zeros_like(named)
    for k in range(nctx):
        named[k, 0:used, :] = tally[k * used : (k + 1) * used]

    r_out = lax.broadcasted_iota(jnp.int32, (rows, rows), 0)
    r_in = lax.broadcasted_iota(jnp.int32, (rows, rows), 1)
    per = rows // nhead
    order = jnp.where(r_in == lax.rem(r_out, per) * nhead + r_out // per, 1.0, 0.0).astype(BF16)
    small[1].wait()
    qsend[...] = jnp.dot(order, queries[...], preferred_element_type=F32).astype(BF16).reshape(nhead, per, width)

    small[2].wait()
    small[3].wait()
    small[4].wait()
    picks = sel.shape[1]
    hi_rows = lax.broadcasted_iota(jnp.int32, (high_rows, picks), 0)
    lo_rows = lax.broadcasted_iota(jnp.int32, (128, picks), 0)
    bits = jnp.zeros((high_rows, 128), jnp.int32)
    for s in range(steps):
        chosen = sel[s : s + 1, :]
        hi_hot = (hi_rows == lax.shift_right_logical(chosen, 7)).astype(F32).astype(BF16)
        lo_hot = (lo_rows == (chosen & 127)).astype(F32).astype(BF16)
        found = lax.dot_general(hi_hot, lo_hot, NT, preferred_element_type=F32)
        bits = bits + jnp.where(found > 0.5, 1 << s, 0)
    member[...] = bits

    loads[0].wait()
    loads[1].wait()
    segment(0, 4)

    nblk = blocks.shape[1]
    lane = lax.broadcasted_iota(jnp.int32, (16, 128), 1)
    sub = lax.broadcasted_iota(jnp.int32, (16, 128), 0)
    spread = sub * 8 + lane // 16
    expanded = []
    for q in range(nblk // 128):
        source = jnp.broadcast_to(blocks[:, q * 128 : (q + 1) * 128], (16, 128))
        expanded.append(jnp.take_along_axis(source, spread, axis=1, mode="promise_in_bounds"))
    dense = jnp.concatenate([ids] + expanded, axis=0)
    hi, lo = lax.shift_right_logical(dense, 7), dense & 127
    seen = jnp.zeros(dense.shape, jnp.int32)
    for r in range(high_rows):
        row = jnp.broadcast_to(bits[r : r + 1, :], dense.shape)
        seen = jnp.where(hi == r, jnp.take_along_axis(row, lo, axis=1, mode="promise_in_bounds"), seen)
    wide = TILE // 128
    mask_of = lax.shift_left(jnp.ones((share, 128), jnp.int32), sub // (share // steps))
    for n in range(tiles):
        for u in range(wide):
            picked = jnp.broadcast_to(seen[n * wide + u : n * wide + u + 1, :], (share, 128)) & mask_of
            bias[n, :, u * 128 : (u + 1) * 128] = jnp.where(picked != 0, 0.0, MASKED)

    pl.semaphore_wait(barrier, nctx - 1 + nhead - 1)
    sibling(0).start()
    each(nhead, lambda k: query_copy(k).start())
    qrecv[head] = qsend[head]
    segment(1, 3)
    segment(2, 5)
    sibling(1).start()
    sibling(2).start()
    start_ring()
    segment(3, 2)
    segment(4, 6)
    sibling(3).start()
    sibling(4).start()
    forward(1, 3, 0, 1)
    forward(2, 5, 1, 1)

    all_queries().wait_recv()
    q = qrecv[...].reshape(rows, width)
    factor = width**-0.5 * LOG2E
    mrun[...] = jnp.full(mrun.shape, FLOOR, F32)

    def score(n, _):
        keys = kv[pl.ds(pl.multiple_of(n * TILE, TILE), TILE), 0:width]
        raw = lax.dot_general(q, keys, NT, preferred_element_type=F32) * factor
        masked = (raw.reshape(nctx, share, TILE) + bias[n][None]).reshape(rows, TILE)
        scores[n] = masked
        top = masked[:, 0:128]
        for u in range(1, wide):
            top = jnp.maximum(top, masked[:, u * 128 : (u + 1) * 128])
        mrun[...] = jnp.maximum(mrun[...], top)
        return 0

    loads[2].wait()
    loads[3].wait()
    lax.fori_loop(0, tiles // 2, score, 0)

    segment(5, 1)
    segment(6, 7)
    sibling(5).start()
    sibling(6).start()
    forward(3, 2, 0, 2)
    forward(4, 6, 1, 2)
    lax.fori_loop(tiles // 2, tiles, score, 0)
    segment(7, 0)
    sibling(7).start()
    forward(5, 1, 0, 3)
    forward(6, 7, 1, 3)

    top_here = jnp.max(mrun[...], axis=1, keepdims=True)
    mrun[...] = jnp.broadcast_to(top_here, mrun.shape)
    lrun[...] = jnp.zeros_like(lrun)
    acc[...] = jnp.zeros_like(acc)

    def weigh(n, _):
        top = mrun[...]
        pieces, total = [], lrun[...]
        for u in range(wide):
            p = jnp.exp2(scores[n, :, u * 128 : (u + 1) * 128] - top)
            total = total + p
            pieces.append(p.astype(BF16))
        lrun[...] = total
        values = kv[pl.ds(pl.multiple_of(n * TILE, TILE), TILE), width : 2 * width]
        acc[...] += jnp.dot(jnp.concatenate(pieces, axis=1), values, preferred_element_type=F32)
        return 0

    lax.fori_loop(0, tiles, weigh, 0)
    total_here = jnp.sum(lrun[...], axis=1, keepdims=True)

    loads[4].wait()
    loads[5].wait()
    sibling(7).wait_recv()
    ends = [(0, 3), (1, 3)]
    key_sums, added = mixed(7, 0, 0, ends)
    value_sums, _ = mixed(7, 0, 1, ends)
    added = added[0:used]
    before = old_counts[pl.ds(me * used, used), :]
    after = before + added
    diagonal = lax.broadcasted_iota(jnp.int32, (128, 128), 0) == lax.broadcasted_iota(jnp.int32, (128, 128), 1)

    def column(x):
        return jnp.concatenate(
            [jnp.sum(jnp.where(diagonal, x[u : u + 1, :], 0.0), axis=1, keepdims=True) for u in range(used)], axis=0
        )

    before_col, after_col = column(before), column(after)
    for u in range(used):
        out_n[:, u * 128 : (u + 1) * 128] = after[u : u + 1, :]
    log_counts = jnp.log(after) * LOG2E
    centre_bias = []
    own_bits = member[pl.ds(me * used, used), :]
    for u in range(used):
        picked = jnp.broadcast_to(own_bits[u : u + 1, :], (share, 128)) & mask_of
        centre_bias.append(jnp.where(picked != 0, MASKED, 0.0) + log_counts[u : u + 1, :])
    centre_bias = jnp.concatenate(centre_bias, axis=1)

    new = []
    for half, out, sums in ((0, out_k, key_sums), (1, out_v, value_sums)):
        value = (before_col * cen[half] + sums) / after_col
        out[...] = value
        new.append(value)

    k_high, k_mid, k_low = split3(new[0])
    raw = lax.dot_general(q, k_low, NT, preferred_element_type=F32)
    raw = raw + lax.dot_general(q, k_mid, NT, preferred_element_type=F32)
    raw = raw + lax.dot_general(q, k_high, NT, preferred_element_type=F32)
    centre = ((raw * factor).reshape(nctx, share, owned) + centre_bias[None]).reshape(rows, owned)
    top_centre = jnp.max(centre, axis=1, keepdims=True)
    top = jnp.maximum(top_here, top_centre)
    weights = jnp.exp2(centre - top)
    w_high, w_low = split2(weights)
    v_high, v_low = split2(new[1])
    gathered = jnp.dot(w_low, v_high, preferred_element_type=F32)
    gathered = gathered + jnp.dot(w_high, v_low, preferred_element_type=F32)
    gathered = gathered + jnp.dot(w_high, v_high, preferred_element_type=F32)
    rescale = jnp.exp2(top_here - top)
    whole = jnp.maximum(jnp.sum(weights, axis=1, keepdims=True) + rescale * total_here, 1e-30)
    result = (gathered + rescale * acc[...]) / whole
    lse = top + jnp.log(whole) * LOG2E

    fsend[:, 0:share, :] = result.astype(BF16).reshape(nctx, share, width)
    spot = lax.broadcasted_iota(jnp.int32, (rows, 128), 1)
    high, mid, low = (x.astype(F32) for x in split3(lse))
    three = jnp.where(spot == 0, high, jnp.where(spot == 1, mid, jnp.where(spot == 2, low, 0.0)))
    fsend[:, share:, :] = three.astype(BF16).reshape(nctx, share, 128)
    half = nctx // 2
    row_copy(half).start()
    for k in range(1, half):
        row_copy(half - k).start()
        row_copy(half + k).start()
    frecv[me] = fsend[me]
    for copy in hops:
        copy.wait_send()
    for j in range(nz):
        sibling(j).wait_send()
    all_queries().wait_send()
    all_rows().wait_recv()
    logs = jnp.sum(frecv[:, share:, :].astype(F32), axis=2, keepdims=True)
    factors = jnp.exp2(logs - jnp.max(logs, axis=0, keepdims=True))
    final = jnp.sum(factors * frecv[:, 0:share, :].astype(F32), axis=0) / jnp.sum(factors, axis=0)
    out_a[...] = final.astype(BF16)
    all_rows().wait_send()


def finish_kernel(k_in, v_in, n_in, a_in, k_out, v_out, n_out, a_out):
    for source, target in ((k_in, k_out), (v_in, v_out), (n_in, n_out), (a_in, a_out)):
        target[...] = source[...]


def shards(
    stretch_keys,
    stretch_values,
    stretch_assign,
    centroid_keys,
    centroid_values,
    cluster_counts,
    cache_keys,
    cache_values,
    block_cluster,
    selected,
    queries,
):
    nctx, nhead = lax.axis_size("ctx"), lax.axis_size("head")
    clusters, width = centroid_keys.shape[1:]
    owned = clusters // nctx
    tokens, cached = stretch_keys.shape[1], cache_keys.shape[1]
    steps, qrows = queries.shape[:2]
    rows = steps * qrows * nhead
    share = rows // nctx
    nz = nctx // 2
    tiles = (tokens + cached) // TILE
    vmem = pl.BlockSpec(memory_space=pltpu.VMEM)
    hbm = pl.BlockSpec(memory_space=pltpu.HBM)
    dma = pltpu.SemaphoreType.DMA
    shapes = (
        jax.ShapeDtypeStruct((owned, width), F32),
        jax.ShapeDtypeStruct((owned, width), F32),
        jax.ShapeDtypeStruct((1, owned), F32),
        jax.ShapeDtypeStruct((share, width), BF16),
    )
    results = pl.pallas_call(
        functools.partial(kernel, nctx, nhead, owned, steps, width),
        out_shape=shapes,
        in_specs=[hbm] * 11,
        out_specs=(vmem,) * 4,
        scratch_shapes=[
            pltpu.VMEM((steps, selected.shape[2]), jnp.int32),
            pltpu.VMEM((tokens // 128, 128), jnp.int32),
            pltpu.VMEM(block_cluster.shape, jnp.int32),
            pltpu.VMEM((clusters // 128, 128), F32),
            pltpu.VMEM((rows, width), BF16),
            pltpu.VMEM((tokens + cached, 2 * width), BF16),
            pltpu.VMEM((2, owned, width), F32),
            pltpu.VMEM((clusters // 128, 128), jnp.int32),
            pltpu.VMEM((tiles, share, TILE), F32),
            pltpu.VMEM((tiles, rows, TILE), F32),
            pltpu.VMEM((rows, 128), F32),
            pltpu.VMEM((rows, width), F32),
            pltpu.VMEM((rows, 128), F32),
            pltpu.VMEM((2, tokens // 128, 128), F32),
            pltpu.VMEM((nz, owned, 2 * width), F32),
            pltpu.VMEM((nz, owned + 16, 2 * width), BF16),
            pltpu.VMEM((nz, owned + 16, 2 * width), BF16),
            pltpu.VMEM((16, owned + 16, width), BF16),
            pltpu.VMEM((16, owned + 16, width), BF16),
            pltpu.VMEM((nhead, rows // nhead, width), BF16),
            pltpu.VMEM((nhead, rows // nhead, width), BF16),
            pltpu.VMEM((nctx, 8, 128), F32),
            pltpu.VMEM((nctx, 2 * share, width), BF16),
            pltpu.VMEM((nctx, 2 * share, width), BF16),
            dma((11,)),
            dma(()), dma(()), dma((nz,)), dma((nz,)), dma((16,)), dma((16,)), dma(()), dma(()),
        ],
        compiler_params=pltpu.CompilerParams(
            collective_id=0, has_side_effects=True, vmem_limit_bytes=60000000
        ),
        name="retrieve",
    )(
        selected.reshape(steps, selected.shape[2]),
        stretch_assign.reshape(tokens // 128, 128),
        block_cluster,
        cluster_counts.reshape(clusters // 128, 128),
        queries.reshape(rows, width),
        stretch_keys, stretch_values, cache_keys, cache_values, centroid_keys, centroid_values,
    )
    new_keys, new_values, new_counts, attended = pl.pallas_call(
        finish_kernel,
        out_shape=shapes,
        in_specs=[vmem] * 4,
        out_specs=(vmem,) * 4,
        name="finish",
    )(*results)
    return (
        new_keys[None],
        new_values[None],
        new_counts,
        attended.reshape(steps, 1, share // steps, width),
    )


def solution(mesh):
    in_specs = (
        P("head", "ctx", None),
        P("head", "ctx", None),
        P("head", "ctx"),
        P("head", None, None),
        P("head", None, None),
        P("head", None),
        P("head", "ctx", None),
        P("head", "ctx", None),
        P("head", "ctx"),
        P(None, "head", None),
        P(None, "head", None, None),
    )
    out_specs = (
        P("head", "ctx", None),
        P("head", "ctx", None),
        P("head", "ctx"),
        P(None, "head", "ctx", None),
    )
    return jax.shard_map(shards, mesh=mesh, in_specs=in_specs, out_specs=out_specs, check_vma=False)
```

```python
import functools
import math

import jax
import jax.numpy as jnp
from jax import lax
from jax.experimental import pallas as pl
from jax.experimental.pallas import tpu as pltpu
from jax.sharding import PartitionSpec as P

MESH = pl.DeviceIdType.MESH
F32 = jnp.float32
BF16 = jnp.bfloat16
LOG2E = math.log2(math.e)
MASKED = -1e30
FLOOR = -1e29
TILE = 3072
NT = (((1,), (1,)), ((), ()))


def split2(x):
    high = x.astype(BF16)
    return high, (x - high.astype(F32)).astype(BF16)


def split3(x):
    high = x.astype(BF16)
    rest = x - high.astype(F32)
    mid = rest.astype(BF16)
    return high, mid, (rest - mid.astype(F32)).astype(BF16)


def kernel(
    nctx, nhead, owned, steps, width,
    sel_in, assign_in, blocks_in, counts_in, queries_in, skeys, svals, ckeys, cvals, cent_k, cent_v,
    out_k, out_v, out_n, out_a,
    sel, assign, blocks, old_counts, queries, kv, cen, member, bias, scores, mrun, acc, lrun, rel, own,
    sib_send, sib_recv, ring_send, ring_recv, qsend, qrecv, named, fsend, frecv,
    load_sem, q_ss, q_rs, s_ss, s_rs, r_ss, r_rs, f_ss, f_rs,
):
    me = lax.axis_index("ctx")
    head = lax.axis_index("head")
    z, core = me // 2, lax.rem(me, 2)
    nz = nctx // 2
    tokens = skeys.shape[1]
    cached = ckeys.shape[1]
    rows = queries_in.shape[0]
    share = rows // nctx
    stretch_tiles = tokens // TILE
    tiles = (tokens + cached) // TILE

    loads = [
        pltpu.make_async_copy(skeys.at[0], kv.at[pl.ds(0, tokens), pl.ds(0, width)], load_sem.at[0]),
        pltpu.make_async_copy(svals.at[0], kv.at[pl.ds(0, tokens), pl.ds(width, width)], load_sem.at[1]),
        pltpu.make_async_copy(ckeys.at[0], kv.at[pl.ds(tokens, cached), pl.ds(0, width)], load_sem.at[2]),
        pltpu.make_async_copy(cvals.at[0], kv.at[pl.ds(tokens, cached), pl.ds(width, width)], load_sem.at[3]),
        pltpu.make_async_copy(cent_k.at[0, pl.ds(me * owned, owned), :], cen.at[0], load_sem.at[4]),
        pltpu.make_async_copy(cent_v.at[0, pl.ds(me * owned, owned), :], cen.at[1], load_sem.at[5]),
    ]
    small = [
        pltpu.make_async_copy(source, target, load_sem.at[6 + n])
        for n, (source, target) in enumerate(
            ((assign_in, assign), (queries_in, queries), (sel_in, sel), (blocks_in, blocks), (counts_in, old_counts))
        )
    ]
    small[0].start()
    loads[0].start()
    loads[1].start()
    for load in small[1:] + loads[2:]:
        load.start()

    barrier = pltpu.get_barrier_semaphore()

    def greet(k, _):
        pl.semaphore_signal(barrier, inc=1, device_id={"ctx": lax.rem(me + k, nctx)}, device_id_type=MESH)
        return 0

    def greet_heads(k, _):
        pl.semaphore_signal(barrier, inc=1, device_id={"head": lax.rem(head + k, nhead)}, device_id_type=MESH)
        return 0

    lax.fori_loop(1, nctx, greet, 0)
    lax.fori_loop(1, nhead, greet_heads, 0)

    small[0].wait()
    ids = assign[...]

    iota = lax.broadcasted_iota(jnp.int32, (owned, width), 0).astype(F32).astype(BF16)
    iota = iota.reshape(owned // 16, 16, width)

    def counts_out(value):
        high = jnp.floor(value * (1 / 256))
        return jnp.concatenate([value - 256 * high, high], axis=0).astype(BF16)

    def counts_in(tile):
        tile = tile.astype(F32)
        return tile[0:8] + 256 * tile[8:16]

    def segment(j, offset):
        zd = lax.rem(z + offset, nz)
        rel[0] = (ids - owned * (2 * zd + 1 - core)).astype(F32)
        rel[1] = (ids - owned * (2 * zd + core)).astype(F32)
        hot = []
        for side in range(2):
            pieces = []
            for u in range(tokens // 128):
                row = jnp.broadcast_to(rel[side, u : u + 1, :], (16, 128)).astype(BF16)
                equal = iota == row[None]
                pieces.append(jnp.where(equal, jnp.ones((), BF16), jnp.zeros((), BF16)).reshape(owned, 128))
            hot.append(jnp.concatenate(pieces, axis=1))
        sums = jnp.dot(jnp.concatenate(hot, axis=0), kv[0:tokens, :], preferred_element_type=F32)
        sib_send[j, 0:owned, :] = sums[0:owned].astype(BF16)
        sib_send[j, owned:, 0:width] = counts_out(named[2 * zd + 1 - core])
        sib_send[j, owned:, width:] = jnp.zeros((16, width), BF16)
        own[j] = sums[owned : 2 * owned]

    def sibling(j):
        return pltpu.make_async_remote_copy(
            sib_send.at[j], sib_recv.at[j], s_ss.at[j], s_rs.at[j],
            device_id={"ctx": 2 * z + 1 - core}, device_id_type=MESH,
        )

    def hop(direction, step, half):
        at = (direction * 4 + step) * 2 + half
        to = lax.rem(z + (1 if direction == 0 else nz - 1), nz)
        length = owned + (16 if half == 0 else 0)
        return pltpu.make_async_remote_copy(
            ring_send.at[at, pl.ds(0, length), :], ring_recv.at[at, pl.ds(0, length), :], r_ss.at[at], r_rs.at[at],
            device_id={"ctx": 2 * to + core}, device_id_type=MESH,
        )

    def mixed(j, offset, half, arrivals):
        columns = slice(half * width, (half + 1) * width)
        value = own[j, :, columns] + sib_recv[j, 0:owned, columns].astype(F32)
        count = None
        if half == 0:
            count = named[2 * lax.rem(z + offset, nz) + core] + counts_in(sib_recv[j, owned:, 0:width])
        for direction, step in arrivals:
            at = (direction * 4 + step) * 2 + half
            value = value + ring_recv[at, 0:owned, :].astype(F32)
            if half == 0:
                count = count + counts_in(ring_recv[at, owned:, :])
        return value, count

    hops = []

    def forward(*moves):
        plans = []
        for j, offset, direction, step in moves:
            first = direction
            for half in (first, 1 - first) if step > 0 else (first,):
                arrivals = [(direction, step - 1)] if step >= 2 or (step == 1 and half == first) else []
                plans.append((j, offset, direction, step, half, arrivals))
        for j in sorted({move[0] for move in moves}):
            sibling(j).wait_recv()
        for _, _, _, _, half, arrivals in plans:
            for direction, step in arrivals:
                hop(direction, step, half).wait_recv()
        for j, offset, direction, step, half, arrivals in plans:
            at = (direction * 4 + step) * 2 + half
            value, count = mixed(j, offset, half, arrivals)
            ring_send[at, 0:owned, :] = value.astype(BF16)
            if half == 0:
                ring_send[at, owned:, :] = counts_out(count)
        for _, _, direction, step, half, _ in plans:
            copy = hop(direction, step, half)
            copy.start()
            hops.append(copy)

    def query_copy(k):
        to = lax.rem(head + k, nhead)
        return pltpu.make_async_remote_copy(
            qsend.at[to], qrecv.at[head], q_ss, q_rs, device_id={"head": to}, device_id_type=MESH
        )

    def row_copy(k):
        to = lax.rem(me + k, nctx)
        return pltpu.make_async_remote_copy(
            fsend.at[to], frecv.at[me], f_ss, f_rs, device_id={"ctx": to}, device_id_type=MESH
        )

    def all_queries():
        part = pl.ds(0, nhead - 1)
        return pltpu.make_async_remote_copy(
            qsend.at[part], qrecv.at[part], q_ss, q_rs, device_id={"head": lax.rem(head + 1, nhead)}, device_id_type=MESH
        )

    def all_rows():
        part = pl.ds(0, nctx - 1)
        return pltpu.make_async_remote_copy(
            fsend.at[part], frecv.at[part], f_ss, f_rs, device_id={"ctx": lax.rem(me + 1, nctx)}, device_id_type=MESH
        )

    def each(count, act):
        def step(k, _):
            act(k)
            return 0

        lax.fori_loop(1, count, step, 0)

    used = owned // 128
    high_rows = nctx * used
    pattern = lax.broadcasted_iota(jnp.int32, (high_rows, 128), 0).astype(F32).astype(BF16)
    pattern = pattern.reshape(high_rows // 16, 16, 128)
    lanes = lax.broadcasted_iota(jnp.int32, (128, 128), 0).astype(F32).astype(BF16).reshape(8, 16, 128)
    rel[0] = lax.shift_right_logical(ids, 7).astype(F32)
    rel[1] = (ids & 127).astype(F32)
    both = []
    for side, table in ((0, pattern), (1, lanes)):
        pieces = []
        for u in range(tokens // 128):
            row = jnp.broadcast_to(rel[side, u : u + 1, :], (16, 128)).astype(BF16)
            equal = table == row[None]
            pieces.append(jnp.where(equal, jnp.ones((), BF16), jnp.zeros((), BF16)).reshape(-1, 128))
        both.append(jnp.concatenate(pieces, axis=1))
    tally = lax.dot_general(both[0], both[1], NT, preferred_element_type=F32)
    named[...] = jnp.zeros_like(named)
    for k in range(nctx):
        named[k, 0:used, :] = tally[k * used : (k + 1) * used]

    r_out = lax.broadcasted_iota(jnp.int32, (rows, rows), 0)
    r_in = lax.broadcasted_iota(jnp.int32, (rows, rows), 1)
    per = rows // nhead
    order = jnp.where(r_in == lax.rem(r_out, per) * nhead + r_out // per, 1.0, 0.0).astype(BF16)
    small[1].wait()
    qsend[...] = jnp.dot(order, queries[...], preferred_element_type=F32).astype(BF16).reshape(nhead, per, width)

    small[2].wait()
    small[3].wait()
    small[4].wait()
    picks = sel.shape[1]
    hi_rows = lax.broadcasted_iota(jnp.int32, (high_rows, picks), 0)
    lo_rows = lax.broadcasted_iota(jnp.int32, (128, picks), 0)
    bits = jnp.zeros((high_rows, 128), jnp.int32)
    for s in range(steps):
        chosen = sel[s : s + 1, :]
        hi_hot = (hi_rows == lax.shift_right_logical(chosen, 7)).astype(F32).astype(BF16)
        lo_hot = (lo_rows == (chosen & 127)).astype(F32).astype(BF16)
        found = lax.dot_general(hi_hot, lo_hot, NT, preferred_element_type=F32)
        bits = bits + jnp.where(found > 0.5, 1 << s, 0)
    member[...] = bits

    loads[0].wait()
    loads[1].wait()
    segment(0, 4)

    nblk = blocks.shape[1]
    lane = lax.broadcasted_iota(jnp.int32, (16, 128), 1)
    sub = lax.broadcasted_iota(jnp.int32, (16, 128), 0)
    spread = sub * 8 + lane // 16
    expanded = []
    for q in range(nblk // 128):
        source = jnp.broadcast_to(blocks[:, q * 128 : (q + 1) * 128], (16, 128))
        expanded.append(jnp.take_along_axis(source, spread, axis=1, mode="promise_in_bounds"))
    dense = jnp.concatenate([ids] + expanded, axis=0)
    hi, lo = lax.shift_right_logical(dense, 7), dense & 127
    seen = jnp.zeros(dense.shape, jnp.int32)
    for r in range(high_rows):
        row = jnp.broadcast_to(bits[r : r + 1, :], dense.shape)
        seen = jnp.where(hi == r, jnp.take_along_axis(row, lo, axis=1, mode="promise_in_bounds"), seen)
    wide = TILE // 128
    mask_of = lax.shift_left(jnp.ones((share, 128), jnp.int32), sub // (share // steps))
    for n in range(tiles):
        for u in range(wide):
            picked = jnp.broadcast_to(seen[n * wide + u : n * wide + u + 1, :], (share, 128)) & mask_of
            bias[n, :, u * 128 : (u + 1) * 128] = jnp.where(picked != 0, 0.0, MASKED)

    pl.semaphore_wait(barrier, nctx - 1 + nhead - 1)
    sibling(0).start()
    segment(1, 3)
    segment(2, 5)
    sibling(1).start()
    sibling(2).start()
    forward((0, 4, 0, 0), (0, 4, 1, 0))
    each(nhead, lambda k: query_copy(k).start())
    qrecv[head] = qsend[head]
    segment(3, 2)
    segment(4, 6)
    sibling(3).start()
    sibling(4).start()
    forward((1, 3, 0, 1), (2, 5, 1, 1))

    all_queries().wait_recv()
    q = qrecv[...].reshape(rows, width)
    factor = width**-0.5 * LOG2E
    mrun[...] = jnp.full(mrun.shape, FLOOR, F32)

    def score(n, _):
        keys = kv[pl.ds(pl.multiple_of(n * TILE, TILE), TILE), 0:width]
        raw = lax.dot_general(q, keys, NT, preferred_element_type=F32) * factor
        masked = (raw.reshape(nctx, share, TILE) + bias[n][None]).reshape(rows, TILE)
        scores[n] = masked
        top = masked[:, 0:128]
        for u in range(1, wide):
            top = jnp.maximum(top, masked[:, u * 128 : (u + 1) * 128])
        mrun[...] = jnp.maximum(mrun[...], top)
        return 0

    loads[2].wait()
    loads[3].wait()
    lax.fori_loop(0, tiles // 2, score, 0)

    segment(5, 1)
    segment(6, 7)
    sibling(5).start()
    sibling(6).start()
    forward((3, 2, 0, 2), (4, 6, 1, 2))
    lax.fori_loop(tiles // 2, tiles, score, 0)
    segment(7, 0)
    sibling(7).start()
    forward((5, 1, 0, 3), (6, 7, 1, 3))

    top_here = jnp.max(mrun[...], axis=1, keepdims=True)
    mrun[...] = jnp.broadcast_to(top_here, mrun.shape)
    lrun[...] = jnp.zeros_like(lrun)
    acc[...] = jnp.zeros_like(acc)

    def weigh(n, _):
        top = mrun[...]
        pieces, total = [], lrun[...]
        for u in range(wide):
            p = jnp.exp2(scores[n, :, u * 128 : (u + 1) * 128] - top)
            total = total + p
            pieces.append(p.astype(BF16))
        lrun[...] = total
        values = kv[pl.ds(pl.multiple_of(n * TILE, TILE), TILE), width : 2 * width]
        acc[...] += jnp.dot(jnp.concatenate(pieces, axis=1), values, preferred_element_type=F32)
        return 0

    lax.fori_loop(0, tiles, weigh, 0)
    total_here = jnp.sum(lrun[...], axis=1, keepdims=True)

    loads[4].wait()
    loads[5].wait()
    sibling(7).wait_recv()
    ends = [(0, 3), (1, 3)]
    for direction, step in ends:
        for half in (0, 1):
            hop(direction, step, half).wait_recv()
    key_sums, added = mixed(7, 0, 0, ends)
    value_sums, _ = mixed(7, 0, 1, ends)
    added = added[0:used]
    before = old_counts[pl.ds(me * used, used), :]
    after = before + added
    diagonal = lax.broadcasted_iota(jnp.int32, (128, 128), 0) == lax.broadcasted_iota(jnp.int32, (128, 128), 1)

    def column(x):
        return jnp.concatenate(
            [jnp.sum(jnp.where(diagonal, x[u : u + 1, :], 0.0), axis=1, keepdims=True) for u in range(used)], axis=0
        )

    before_col, after_col = column(before), column(after)
    for u in range(used):
        out_n[:, u * 128 : (u + 1) * 128] = after[u : u + 1, :]
    log_counts = jnp.log(after) * LOG2E
    centre_bias = []
    own_bits = member[pl.ds(me * used, used), :]
    for u in range(used):
        picked = jnp.broadcast_to(own_bits[u : u + 1, :], (share, 128)) & mask_of
        centre_bias.append(jnp.where(picked != 0, MASKED, 0.0) + log_counts[u : u + 1, :])
    centre_bias = jnp.concatenate(centre_bias, axis=1)

    new = []
    for half, out, sums in ((0, out_k, key_sums), (1, out_v, value_sums)):
        value = (before_col * cen[half] + sums) / after_col
        out[...] = value
        new.append(value)

    k_high, k_mid, k_low = split3(new[0])
    raw = lax.dot_general(q, k_low, NT, preferred_element_type=F32)
    raw = raw + lax.dot_general(q, k_mid, NT, preferred_element_type=F32)
    raw = raw + lax.dot_general(q, k_high, NT, preferred_element_type=F32)
    centre = ((raw * factor).reshape(nctx, share, owned) + centre_bias[None]).reshape(rows, owned)
    top_centre = jnp.max(centre, axis=1, keepdims=True)
    top = jnp.maximum(top_here, top_centre)
    weights = jnp.exp2(centre - top)
    w_high, w_low = split2(weights)
    v_high, v_low = split2(new[1])
    gathered = jnp.dot(w_low, v_high, preferred_element_type=F32)
    gathered = gathered + jnp.dot(w_high, v_low, preferred_element_type=F32)
    gathered = gathered + jnp.dot(w_high, v_high, preferred_element_type=F32)
    rescale = jnp.exp2(top_here - top)
    whole = jnp.maximum(jnp.sum(weights, axis=1, keepdims=True) + rescale * total_here, 1e-30)
    result = (gathered + rescale * acc[...]) / whole
    lse = top + jnp.log(whole) * LOG2E

    fsend[:, 0:share, :] = result.astype(BF16).reshape(nctx, share, width)
    spot = lax.broadcasted_iota(jnp.int32, (rows, 128), 1)
    high, mid, low = (x.astype(F32) for x in split3(lse))
    three = jnp.where(spot == 0, high, jnp.where(spot == 1, mid, jnp.where(spot == 2, low, 0.0)))
    fsend[:, share:, :] = three.astype(BF16).reshape(nctx, share, 128)
    half = nctx // 2
    row_copy(half).start()
    for k in range(1, half):
        row_copy(half - k).start()
        row_copy(half + k).start()
    frecv[me] = fsend[me]
    for copy in hops:
        copy.wait_send()
    for j in range(nz):
        sibling(j).wait_send()
    all_queries().wait_send()
    all_rows().wait_recv()
    logs = jnp.sum(frecv[:, share:, :].astype(F32), axis=2, keepdims=True)
    factors = jnp.exp2(logs - jnp.max(logs, axis=0, keepdims=True))
    final = jnp.sum(factors * frecv[:, 0:share, :].astype(F32), axis=0) / jnp.sum(factors, axis=0)
    out_a[...] = final.astype(BF16)
    all_rows().wait_send()


def finish_kernel(k_in, v_in, n_in, a_in, k_out, v_out, n_out, a_out):
    for source, target in ((k_in, k_out), (v_in, v_out), (n_in, n_out), (a_in, a_out)):
        target[...] = source[...]


def shards(
    stretch_keys,
    stretch_values,
    stretch_assign,
    centroid_keys,
    centroid_values,
    cluster_counts,
    cache_keys,
    cache_values,
    block_cluster,
    selected,
    queries,
):
    nctx, nhead = lax.axis_size("ctx"), lax.axis_size("head")
    clusters, width = centroid_keys.shape[1:]
    owned = clusters // nctx
    tokens, cached = stretch_keys.shape[1], cache_keys.shape[1]
    steps, qrows = queries.shape[:2]
    rows = steps * qrows * nhead
    share = rows // nctx
    nz = nctx // 2
    tiles = (tokens + cached) // TILE
    vmem = pl.BlockSpec(memory_space=pltpu.VMEM)
    hbm = pl.BlockSpec(memory_space=pltpu.HBM)
    dma = pltpu.SemaphoreType.DMA
    shapes = (
        jax.ShapeDtypeStruct((owned, width), F32),
        jax.ShapeDtypeStruct((owned, width), F32),
        jax.ShapeDtypeStruct((1, owned), F32),
        jax.ShapeDtypeStruct((share, width), BF16),
    )
    results = pl.pallas_call(
        functools.partial(kernel, nctx, nhead, owned, steps, width),
        out_shape=shapes,
        in_specs=[hbm] * 11,
        out_specs=(vmem,) * 4,
        scratch_shapes=[
            pltpu.VMEM((steps, selected.shape[2]), jnp.int32),
            pltpu.VMEM((tokens // 128, 128), jnp.int32),
            pltpu.VMEM(block_cluster.shape, jnp.int32),
            pltpu.VMEM((clusters // 128, 128), F32),
            pltpu.VMEM((rows, width), BF16),
            pltpu.VMEM((tokens + cached, 2 * width), BF16),
            pltpu.VMEM((2, owned, width), F32),
            pltpu.VMEM((clusters // 128, 128), jnp.int32),
            pltpu.VMEM((tiles, share, TILE), F32),
            pltpu.VMEM((tiles, rows, TILE), F32),
            pltpu.VMEM((rows, 128), F32),
            pltpu.VMEM((rows, width), F32),
            pltpu.VMEM((rows, 128), F32),
            pltpu.VMEM((2, tokens // 128, 128), F32),
            pltpu.VMEM((nz, owned, 2 * width), F32),
            pltpu.VMEM((nz, owned + 16, 2 * width), BF16),
            pltpu.VMEM((nz, owned + 16, 2 * width), BF16),
            pltpu.VMEM((16, owned + 16, width), BF16),
            pltpu.VMEM((16, owned + 16, width), BF16),
            pltpu.VMEM((nhead, rows // nhead, width), BF16),
            pltpu.VMEM((nhead, rows // nhead, width), BF16),
            pltpu.VMEM((nctx, 8, 128), F32),
            pltpu.VMEM((nctx, 2 * share, width), BF16),
            pltpu.VMEM((nctx, 2 * share, width), BF16),
            dma((11,)),
            dma(()), dma(()), dma((nz,)), dma((nz,)), dma((16,)), dma((16,)), dma(()), dma(()),
        ],
        compiler_params=pltpu.CompilerParams(
            collective_id=0, has_side_effects=True, vmem_limit_bytes=60000000
        ),
        name="retrieve",
    )(
        selected.reshape(steps, selected.shape[2]),
        stretch_assign.reshape(tokens // 128, 128),
        block_cluster,
        cluster_counts.reshape(clusters // 128, 128),
        queries.reshape(rows, width),
        stretch_keys, stretch_values, cache_keys, cache_values, centroid_keys, centroid_values,
    )
    new_keys, new_values, new_counts, attended = pl.pallas_call(
        finish_kernel,
        out_shape=shapes,
        in_specs=[vmem] * 4,
        out_specs=(vmem,) * 4,
        name="finish",
    )(*results)
    return (
        new_keys[None],
        new_values[None],
        new_counts,
        attended.reshape(steps, 1, share // steps, width),
    )


def solution(mesh):
    in_specs = (
        P("head", "ctx", None),
        P("head", "ctx", None),
        P("head", "ctx"),
        P("head", None, None),
        P("head", None, None),
        P("head", None),
        P("head", "ctx", None),
        P("head", "ctx", None),
        P("head", "ctx"),
        P(None, "head", None),
        P(None, "head", None, None),
    )
    out_specs = (
        P("head", "ctx", None),
        P("head", "ctx", None),
        P("head", "ctx"),
        P(None, "head", "ctx", None),
    )
    return jax.shard_map(shards, mesh=mesh, in_specs=in_specs, out_specs=out_specs, check_vma=False)
```
